32 devices in a mesh: groups: 2 (over x), seq: 16 (over z, y, core).
Axes of the slice: x: 2, y: 2, z: 4, core: 2. Of those that a mesh axis runs over, the one named last changes fastest.
Arguments:
- moe_input: bfloat16 [4096, 1536], P(('groups', 'seq')), parts along dimension 0, may hold values from -6 to 6
- residual_in: bfloat16 [4096, 1536], P(('groups', 'seq')), parts along dimension 0, may hold values from -3 to 3
- expert_ids: int32 [4096, 4], P(('groups', 'seq')), parts along dimension 0, may hold values from 0 to 15, all different within a row; in each aligned block of 128 rows (0 to 127, 128 to 255, ...) at most 64 rows name the same one
- route_logits: float32 [4096, 4], P(('groups', 'seq')), parts along dimension 0, may hold values from -5 to 5
- kept_blocks: int32 [16, 6], P('seq'), may hold values from 0 to 11, as said below
- w_gate: bfloat16 [16, 1536, 768], P('seq'), may hold values from -0.15625 to 0.15625
- w_up: bfloat16 [16, 1536, 768], P('seq'), may hold values from -0.15625 to 0.15625
- w_down: bfloat16 [16, 768, 1536], P('seq'), may hold values from -0.21875 to 0.21875
- norm_gain: float32 [1536], replicated, may hold values from 0.1 to 1.9
- qkv_weight: bfloat16 [1536, 2560], P('seq'), may hold values from -6 to 6
Outputs:
- attention: bfloat16 [4096, 2048], P(('groups', 'seq')), parts along dimension 0
- neuron_energy: float32 [16, 3072], P('seq', 'groups'), parts along dimension 1
The draws below stay inside these ranges and needn't reach their ends.
There are 2 independent parts, one for each index of `groups`. The reference program is written for one: setup_inputs(seed, part) draws one part's arguments, and reference() takes and returns one part's arrays. A program takes and returns all parts, laid end to end along the dimension named above; an argument that names none is the same for every part. Nothing has to cross between parts.
Inputs may be any that keep to these rules, and one draw needn't show every extreme that they name: `expert_ids`: the 4 experts of a token differ; among the 128 tokens of one device no expert is named more than 64 times, a bound that some block reaches. `kept_blocks`: each row names 6 different blocks in increasing order.
All inputs are finite; a program needn't handle non-finite values.
Results may differ from the reference program's by a relative error of at most 0.0095.
Values may be sent and summed in bfloat16 or wider, within the bound.
A program may use at most 128 MiB of HBM per device.

```python
import math
import jax
import jax.numpy as jnp
import numpy as np
from jax import lax

D = 1536
TOP = 4
BLOCK = 128
KB = 6
OB = 12
QH = 32
KVH = 4
HD = 64
TOK_DEV = 128
EXPERTS = 16
MOST = 64
TOKENS = 2048
KEPT = 768
N_SEQ = 16


def draw_kept_blocks(key, part):
    key = jax.random.fold_in(key, 5)
    ranking_scores = jax.random.randint(key, (EXPERTS, OB), 0, 1 << 20) * OB + jnp.arange(OB, dtype=jnp.int32)[None, :]
    ranking = jnp.argsort(ranking_scores, axis=1)
    return jnp.sort(ranking[:, :KB], axis=1).astype(jnp.int32)


def draw_qkv_weight(key, part):
    key = jax.random.fold_in(key, 9)
    key_base = jax.random.fold_in(key, 0)
    base_draw = jax.random.normal(key_base, (D, QH * HD + 2 * KVH * HD), jnp.float32) * D ** (-0.5)
    return jnp.clip(base_draw, -6.0, 6.0).astype(jnp.bfloat16)


def level_of(stream_key, extent, shards, low, top_value):
    def one(dim, parts):
        draws = jax.random.uniform(jax.random.fold_in(jax.random.fold_in(stream_key, 6), dim), (parts,), jnp.float32, low / len(shards), top_value / len(shards))
        return jnp.repeat(jnp.exp(draws), extent[dim] // parts).reshape((-1,) + (1,) * (len(extent) - dim - 1))

    factor_of = one(*shards[0])
    for cut in shards[1:]:
        factor_of = factor_of * one(*cut)
    return factor_of


def assign_block(stream_key, own, number, rows, number_of, top, reach, slope):
    order = jax.random.permutation(stream_key, number_of)
    heavy_load, usual = portions_of(number_of, rows * top, reach, slope, True), portions_of(number_of, rows * top, reach, slope, False)
    places = jnp.arange(number_of)

    def named(tallies, rotation):
        used = int((tallies > 0).sum())
        fixed = max(1, used // 4)
        moved = fixed + (places - fixed + rotation * (used - fixed)) % max(1, number_of - fixed)
        return jnp.zeros((number_of,), jnp.int32).at[order[jnp.where(places < fixed, places, moved)]].set(jnp.asarray(tallies, jnp.int32))

    tallies = jnp.where(number % 4 == 0, named(heavy_load, number // 4), named(usual, number - number // 4 - 1))
    mixed = jax.random.permutation(jax.random.fold_in(own, 3), number_of)
    source_of, taker = mixed[0:number_of // 2 * 2:2], mixed[1:number_of // 2 * 2:2]
    room = jnp.minimum(tallies[source_of] - 1, reach - tallies[taker]) // 2
    room = jnp.where((source_of == order[0]) | (taker == order[0]) | (tallies[taker] == 0), 0, jnp.maximum(room, 0))
    moved = jax.random.randint(jax.random.fold_in(own, 4), (number_of // 2,), 0, 1 << 20) % (room + 1)
    tallies = tallies.at[source_of].add(-moved).at[taker].add(moved)
    members = jnp.searchsorted(jnp.cumsum(tallies), jnp.arange(rows * top), side="right").astype(jnp.int32)
    listing = members.reshape(top, rows).T
    listing = listing[jax.random.permutation(jax.random.fold_in(own, 1), rows)]
    rotation = jax.random.randint(jax.random.fold_in(own, 2), (rows, 1), 0, top)
    return jnp.take_along_axis(listing, (jnp.arange(top)[None, :] + rotation) % top, axis=1)


def portions_of(number_of, total, bound, slope, full):
    portions = [(1 << 20) // math.isqrt(standing ** slope) + 1 for standing in range(1, number_of + 1)]
    largest = bound if full else min(bound, max(-(-total // number_of), total * portions[0] // sum(portions)))
    least = 1 if total - largest >= number_of - 1 else 0
    holding, rest = [largest] + [least] * (number_of - 1), total - largest - least * (number_of - 1)
    while rest > 0:
        candidates = [i for i in range(1, number_of) if holding[i] < largest] or [i for i in range(1, number_of) if holding[i] < bound]
        pool, remaining = sum([portions[i] for i in candidates]), rest
        for i in candidates:
            addition = min(bound - holding[i], max(1, remaining * portions[i] // pool), rest)
            holding[i] = holding[i] + addition
            rest = rest - addition
    return np.array(holding)


def gaussian(rng, dims, scale, limit, shards=(), kind=jnp.bfloat16):
    drawn = scale * jax.random.normal(rng, dims, jnp.float32)
    if shards:
        drawn = drawn * level_of(rng, dims, shards, -0.22, 0.18)
    return jnp.clip(drawn, -limit, limit).astype(kind)


def setup_inputs(seed: int = 0, part: int = 0) -> dict:
    key_of = jax.random.split(jax.random.key(seed), 11)
    part_keys = jax.random.split(jax.random.fold_in(key_of[10], part), 11)
    moe_input = gaussian(part_keys[0], (TOKENS, D), 1.0, 6.0, ((0, 16),))
    residual_in = gaussian(part_keys[1], (TOKENS, D), 0.5, 3.0, ((0, 16),))
    expert_ids_keys = jax.random.split(jax.random.fold_in(part_keys[2], 1), TOKENS // TOK_DEV)
    expert_ids_turns = jax.random.permutation(jax.random.fold_in(part_keys[2], 3), TOKENS // TOK_DEV)
    expert_ids = jax.vmap(lambda own, number: assign_block(jax.random.fold_in(part_keys[2], 2), own, number, TOK_DEV, EXPERTS, TOP, MOST, 2))(expert_ids_keys, expert_ids_turns).reshape((TOKENS, TOP))
    route_logits = gaussian(part_keys[3], (TOKENS, TOP), 1.0, 5.0, ((0, 16),), jnp.float32)
    kept_blocks = draw_kept_blocks(jax.random.fold_in(key_of[10], 71), part)
    w_gate = gaussian(key_of[5], (EXPERTS, D, KEPT), D ** -0.5, 0.15625, ((0, 16),))
    w_up = gaussian(key_of[6], (EXPERTS, D, KEPT), D ** -0.5, 0.15625, ((0, 16),))
    w_down = gaussian(key_of[7], (EXPERTS, KEPT, D), KEPT ** -0.5, 0.21875, ((0, 16),))
    norm_gain = jnp.clip(1.0 + 0.18 * jax.random.normal(key_of[8], (D,), jnp.float32), 0.1, 1.9)
    qkv_weight = draw_qkv_weight(jax.random.fold_in(key_of[10], 71), part)
    return {"moe_input": moe_input, "residual_in": residual_in, "expert_ids": expert_ids, "route_logits": route_logits, "kept_blocks": kept_blocks, "w_gate": w_gate, "w_up": w_up, "w_down": w_down, "norm_gain": norm_gain, "qkv_weight": qkv_weight}


def expert_rows(token_rows, gate_w, up_w, down_w):
    gate_part = jnp.dot(token_rows, gate_w, preferred_element_type=jnp.float32)
    up_part = jnp.dot(token_rows, up_w, preferred_element_type=jnp.float32)
    hidden = jax.nn.silu(gate_part) * up_part
    result = jnp.dot(hidden.astype(jnp.bfloat16), down_w, preferred_element_type=jnp.float32).astype(jnp.bfloat16)
    return (result, hidden * hidden)

def reference(moe_input, residual_in, expert_ids, route_logits, kept_blocks, w_gate, w_up, w_down, norm_gain, qkv_weight):
    flat_ids = expert_ids.reshape(-1)
    source = jnp.arange(TOKENS * TOP, dtype=jnp.int32) // (TOK_DEV * TOP)
    onehot = (flat_ids[:, None] == jnp.arange(EXPERTS, dtype=jnp.int32)[None, :]).astype(jnp.int32)
    grouped = onehot.reshape(N_SEQ, TOK_DEV * TOP, EXPERTS)
    before = (jnp.cumsum(grouped, axis=1) - grouped).reshape(TOKENS * TOP, EXPERTS)
    slot_index = lax.optimization_barrier(jnp.sum(before * onehot, axis=1)).astype(jnp.int32)
    position = (source * MOST + slot_index).astype(jnp.int32)
    token_rows = jnp.repeat(moe_input, TOP, axis=0)
    raised = jnp.exp(route_logits)
    route_weights = (raised / lax.optimization_barrier(jnp.sum(raised, axis=-1, keepdims=True))).reshape(-1)
    spare_row = N_SEQ * MOST

    def one_expert(running_sum, inputs):
        expert_id, gate_w, up_w, down_w, kept = inputs
        target = jnp.where(flat_ids == expert_id, position, spare_row).astype(jnp.int32)
        buffer = jnp.zeros((spare_row + 1, D), jnp.bfloat16).at[target].set(token_rows)
        result, squares = expert_rows(buffer[:spare_row], gate_w, up_w, down_w)
        result = jnp.concatenate([result, jnp.zeros((1, D), jnp.bfloat16)], axis=0)
        picked = result[target].astype(jnp.float32) * route_weights[:, None]
        running_sum = running_sum + lax.optimization_barrier(jnp.sum(picked.reshape(TOKENS, TOP, D), axis=1))
        energy = jnp.sqrt(lax.optimization_barrier(jnp.sum(squares, axis=0)) / spare_row + 1e-06).reshape(KB, BLOCK)
        placed = jnp.zeros((OB, BLOCK), jnp.float32).at[kept].set(energy).reshape(OB * BLOCK)
        return (running_sum, placed)
    expert_list = jnp.arange(EXPERTS, dtype=jnp.int32)
    moe_sum, neuron_energy = lax.scan(one_expert, jnp.zeros((TOKENS, D), jnp.float32), (expert_list, w_gate, w_up, w_down, kept_blocks))
    mixed = residual_in.astype(jnp.float32) + moe_sum
    normed = (mixed * lax.rsqrt(lax.optimization_barrier(jnp.mean(mixed * mixed, axis=-1, keepdims=True)) + 1e-05) * norm_gain).astype(jnp.bfloat16)
    projected = jnp.dot(normed, qkv_weight, preferred_element_type=jnp.float32).astype(jnp.bfloat16)
    query_block = min(256, TOKENS)
    query_width = QH * HD
    queries = projected[:, :query_width].reshape(TOKENS // query_block, query_block, KVH, QH // KVH, HD)
    key_table = projected[:, query_width:query_width + KVH * HD].reshape(TOKENS, KVH, HD).astype(jnp.float32)
    value_table = projected[:, query_width + KVH * HD:].reshape(TOKENS, KVH, HD).astype(jnp.float32)
    starts = jnp.arange(TOKENS // query_block, dtype=jnp.int32) * query_block

    def attend_block(inputs):
        query_rows, begin_at = inputs
        scores = jnp.einsum('tkgd,skd->kgts', query_rows.astype(jnp.float32), key_table) * HD ** (-0.5)
        query_pos = begin_at + jnp.arange(query_block, dtype=jnp.int32)
        key_pos = jnp.arange(TOKENS, dtype=jnp.int32)
        visible = key_pos[None, :] <= query_pos[:, None]
        scores = jnp.where(visible, scores, -1e+30)
        row_max = lax.optimization_barrier(jnp.max(scores, axis=-1, keepdims=True))
        softmax_p = jnp.where(visible, jnp.exp(scores - row_max), 0.0)
        denom_sum = lax.optimization_barrier(jnp.sum(softmax_p, axis=-1))
        p_round = lax.optimization_barrier(softmax_p.astype(jnp.bfloat16))
        weighted = jnp.einsum('kgts,skd->kgtd', p_round.astype(jnp.float32), value_table)
        output = weighted / denom_sum[..., None]
        return output.transpose(2, 0, 1, 3).reshape(query_block, query_width).astype(jnp.bfloat16)
    attention = lax.map(attend_block, (queries, starts)).reshape(TOKENS, query_width)
    return (attention, neuron_energy)
```

```python
import functools

import jax
import jax.numpy as jnp
from jax import lax
from jax.experimental import pallas as pl
from jax.experimental.pallas import tpu as pltpu
from jax.sharding import PartitionSpec as P

TOP = 4
BLOCK = 128
KB = 6
OB = 12
QH = 32
KVH = 4
HD = 64
BK = 256
QCHUNK = 512
F32 = jnp.float32
BF16 = jnp.bfloat16


def attention_kernel(qt_ref, kv_ref, out_ref, q_scr, m_scr, l_scr, acc_scr):
    me = lax.axis_index("seq")
    tokens = qt_ref.shape[1]
    heads = QCHUNK // tokens
    chunks = QH // heads
    for c in range(chunks):
        for h in range(heads):
            row = (c * heads + h) * HD
            q_scr[c, :, h * tokens : (h + 1) * tokens] = qt_ref[row : row + HD, :]
    m_scr[...] = jnp.full_like(m_scr, -1e30)
    l_scr[...] = jnp.zeros_like(l_scr)
    acc_scr[...] = jnp.zeros_like(acc_scr)

    def block(kb, masked):
        start = pl.multiple_of(kb * BK, BK)
        if masked:
            key_pos = start + lax.broadcasted_iota(jnp.int32, (BK, tokens), 0)
            query_pos = me * tokens + lax.broadcasted_iota(jnp.int32, (BK, tokens), 1)
            hide = jnp.where(key_pos <= query_pos, 0.0, -1e30)
            hide = jnp.concatenate([hide] * heads, axis=1)
        for c in range(chunks):
            g = c * heads // (QH // KVH)
            keys = kv_ref[pl.ds(start, BK), g * HD : (g + 1) * HD]
            vals = kv_ref[pl.ds(start, BK), (KVH + g) * HD : (KVH + g + 1) * HD]
            s = jnp.dot(keys, q_scr[c], preferred_element_type=F32)
            if masked:
                s = s + hide
            m_old = m_scr[c]
            m_new = jnp.maximum(m_old, jnp.max(s, axis=0, keepdims=True))
            p = jnp.exp(s - m_new)
            alpha = jnp.exp(m_old - m_new)
            m_scr[c] = m_new
            l_scr[c] = l_scr[c] * alpha + jnp.sum(p, axis=0, keepdims=True)
            pv = lax.dot_general(
                vals, p.astype(BF16), (((0,), (0,)), ((), ())), preferred_element_type=F32
            )
            acc_scr[c] = acc_scr[c] * alpha + pv

    full = me * tokens // BK

    @pl.loop(0, full)
    def _(kb):
        block(kb, False)

    block(full, True)
    for c in range(chunks):
        o = acc_scr[c] / l_scr[c]
        for h in range(0, heads, 2):
            pair = jnp.concatenate(
                [o[:, h * tokens : (h + 1) * tokens], o[:, (h + 1) * tokens : (h + 2) * tokens]], axis=0
            )
            col = (c * heads + h) * HD
            out_ref[:, col : col + 2 * HD] = pair.T.astype(BF16)


def attention_call(qt, kv):
    tokens = qt.shape[1]
    chunks = QH * tokens // QCHUNK
    return pl.pallas_call(
        attention_kernel,
        out_shape=jax.ShapeDtypeStruct((tokens, QH * HD), BF16),
        in_specs=[pl.BlockSpec(memory_space=pltpu.VMEM)] * 2,
        out_specs=pl.BlockSpec(memory_space=pltpu.VMEM),
        scratch_shapes=[
            pltpu.VMEM((chunks, HD, QCHUNK), BF16),
            pltpu.VMEM((chunks, 1, QCHUNK), F32),
            pltpu.VMEM((chunks, 1, QCHUNK), F32),
            pltpu.VMEM((chunks, HD, QCHUNK), F32),
        ],
        compiler_params=pltpu.CompilerParams(vmem_limit_bytes=40 * 1024 * 1024),
        name="attention",
    )(qt, kv)


def on_device(
    moe_input,
    residual_in,
    expert_ids,
    route_logits,
    kept_blocks,
    w_gate,
    w_up,
    w_down,
    norm_gain,
    qkv_weight,
):
    tokens, width = moe_input.shape
    seq = lax.axis_size("seq")
    me = lax.axis_index("seq")
    cap = min(tokens, max(2, tokens * TOP * 2 // seq))
    raised = jnp.exp(route_logits)
    weights = raised / jnp.sum(raised, axis=-1, keepdims=True)
    meta = jnp.concatenate([expert_ids.astype(F32), weights], axis=1)
    meta = lax.all_gather(meta, "seq", axis=0, tiled=True)
    rows = lax.all_gather(moe_input, "seq", axis=0, tiled=True)
    qkv_full = lax.all_gather(qkv_weight, "seq", axis=0, tiled=True)

    hit = (meta[:, :TOP] == me.astype(F32)).astype(F32)
    share = jnp.sum(hit * meta[:, TOP:], axis=1).reshape(seq, tokens)
    named = jnp.sum(hit, axis=1).reshape(seq, tokens)
    earlier = (jnp.arange(tokens)[:, None] < jnp.arange(tokens)[None, :]).astype(F32)
    slot = jnp.dot(named, earlier)
    slot = jnp.where(named > 0.5, slot, -1.0)
    place = (slot[:, None, :] == jnp.arange(cap, dtype=F32)[None, :, None]).astype(BF16)
    sent = jnp.einsum(
        "sct,std->scd", place, rows.reshape(seq, tokens, width), preferred_element_type=F32
    ).astype(BF16).reshape(seq * cap, width)
    gate_part = jnp.dot(sent, w_gate[0], preferred_element_type=F32)
    up_part = jnp.dot(sent, w_up[0], preferred_element_type=F32)
    hidden = jax.nn.silu(gate_part) * up_part
    energy = jnp.sqrt(jnp.sum(hidden * hidden, axis=0) / (seq * cap) + 1e-06)
    result = jnp.dot(hidden.astype(BF16), w_down[0], preferred_element_type=F32).astype(BF16)
    chosen = (kept_blocks[0][:, None] == jnp.arange(OB, dtype=jnp.int32)[None, :]).astype(F32)
    placed = jnp.einsum(
        "bo,bc->oc", chosen, energy.reshape(KB, BLOCK), precision=lax.Precision.HIGHEST
    )
    neuron_energy = placed.reshape(1, OB * BLOCK)
    back = jnp.einsum(
        "sct,scd->std", place, result.reshape(seq, cap, width), preferred_element_type=F32
    )
    partial = (back * share[..., None]).astype(BF16).reshape(seq * tokens, width)
    moe = lax.psum_scatter(partial, "seq", scatter_dimension=0, tiled=True)
    mixed = residual_in.astype(F32) + moe.astype(F32)
    normed = (
        mixed * lax.rsqrt(jnp.mean(mixed * mixed, axis=-1, keepdims=True) + 1e-05) * norm_gain
    ).astype(BF16)
    query_width = QH * HD
    keys_vals = jnp.dot(normed, qkv_full[:, query_width:], preferred_element_type=F32).astype(BF16)
    kv = lax.all_gather(keys_vals, "seq", axis=0, tiled=True)
    queries = jnp.dot(normed, qkv_full[:, :query_width], preferred_element_type=F32).astype(BF16)
    attention = attention_call((queries * HD ** (-0.5)).T, kv)
    return (attention, neuron_energy)


def solution(mesh):
    return jax.shard_map(
        on_device,
        mesh=mesh,
        in_specs=(
            P(("groups", "seq"), None),
            P(("groups", "seq"), None),
            P(("groups", "seq"), None),
            P(("groups", "seq"), None),
            P("seq", None),
            P("seq", None, None),
            P("seq", None, None),
            P("seq", None, None),
            P(),
            P("seq", None),
        ),
        out_specs=(P(("groups", "seq"), None), P("seq", "groups")),
        check_vma=False,
    )
```

```python
import functools

import jax
import jax.numpy as jnp
from jax import lax
from jax.experimental import pallas as pl
from jax.experimental.pallas import tpu as pltpu
from jax.sharding import PartitionSpec as P

TOP = 4
BLOCK = 128
KB = 6
OB = 12
QH = 32
KVH = 4
HD = 64
BK = 256
QCHUNK = 512
F32 = jnp.float32
BF16 = jnp.bfloat16


def attention_kernel(qt_ref, kv_ref, out_ref, q_scr, m_scr, l_scr, acc_scr):
    me = lax.axis_index("seq")
    tokens = qt_ref.shape[1]
    heads = QCHUNK // tokens
    chunks = QH // heads
    for c in range(chunks):
        for h in range(heads):
            row = (c * heads + h) * HD
            q_scr[c, :, h * tokens : (h + 1) * tokens] = qt_ref[row : row + HD, :]
    m_scr[...] = jnp.full_like(m_scr, -1e30)
    l_scr[...] = jnp.zeros_like(l_scr)
    acc_scr[...] = jnp.zeros_like(acc_scr)

    def block(kb, masked):
        start = pl.multiple_of(kb * BK, BK)
        if masked:
            key_pos = start + lax.broadcasted_iota(jnp.int32, (BK, tokens), 0)
            query_pos = me * tokens + lax.broadcasted_iota(jnp.int32, (BK, tokens), 1)
            hide = jnp.where(key_pos <= query_pos, 0.0, -1e30)
            hide = jnp.concatenate([hide] * heads, axis=1)
        for c in range(chunks):
            g = c * heads // (QH // KVH)
            keys = kv_ref[pl.ds(start, BK), g * HD : (g + 1) * HD]
            vals = kv_ref[pl.ds(start, BK), (KVH + g) * HD : (KVH + g + 1) * HD]
            s = jnp.dot(keys, q_scr[c], preferred_element_type=F32)
            if masked:
                s = s + hide
            m_old = m_scr[c]
            m_new = jnp.maximum(m_old, jnp.max(s, axis=0, keepdims=True))
            p = jnp.exp(s - m_new)
            alpha = jnp.exp(m_old - m_new)
            m_scr[c] = m_new
            l_scr[c] = l_scr[c] * alpha + jnp.sum(p, axis=0, keepdims=True)
            pv = lax.dot_general(
                vals, p.astype(BF16), (((0,), (0,)), ((), ())), preferred_element_type=F32
            )
            acc_scr[c] = acc_scr[c] * alpha + pv

    full = me * tokens // BK

    @pl.loop(0, full)
    def _(kb):
        block(kb, False)

    block(full, True)
    for c in range(chunks):
        o = acc_scr[c] / l_scr[c]
        for h in range(0, heads, 2):
            pair = jnp.concatenate(
                [o[:, h * tokens : (h + 1) * tokens], o[:, (h + 1) * tokens : (h + 2) * tokens]], axis=0
            )
            col = (c * heads + h) * HD
            out_ref[:, col : col + 2 * HD] = pair.T.astype(BF16)


def attention_call(qt, kv):
    tokens = qt.shape[1]
    chunks = QH * tokens // QCHUNK
    return pl.pallas_call(
        attention_kernel,
        out_shape=jax.ShapeDtypeStruct((tokens, QH * HD), BF16),
        in_specs=[pl.BlockSpec(memory_space=pltpu.VMEM)] * 2,
        out_specs=pl.BlockSpec(memory_space=pltpu.VMEM),
        scratch_shapes=[
            pltpu.VMEM((chunks, HD, QCHUNK), BF16),
            pltpu.VMEM((chunks, 1, QCHUNK), F32),
            pltpu.VMEM((chunks, 1, QCHUNK), F32),
            pltpu.VMEM((chunks, HD, QCHUNK), F32),
        ],
        compiler_params=pltpu.CompilerParams(vmem_limit_bytes=40 * 1024 * 1024),
        name="attention",
    )(qt, kv)


MESH = pl.DeviceIdType.MESH


def position():
    me = lax.axis_index("seq")
    return me, me // 4, (me // 2) % 2, me % 2


def at(z, y, c):
    return (z * 2 + y) * 2 + c


def remote(src, dst, send_sem, recv_sem, target):
    return pltpu.make_async_remote_copy(
        src_ref=src,
        dst_ref=dst,
        send_sem=send_sem,
        recv_sem=recv_sem,
        device_id={"seq": target},
        device_id_type=MESH,
    )


def greet(rows):
    me, z, y, c = position()
    barrier = pltpu.get_barrier_semaphore()
    near = (
        at((z + 1) % rows, y, c),
        at((z + rows - 1) % rows, y, c),
        at(z, 1 - y, c),
        at(z, y, 1 - c),
    )
    for target in near:
        pl.semaphore_signal(barrier, inc=1, device_id={"seq": target}, device_id_type=MESH)
    pl.semaphore_wait(barrier, len(near))


def gather_kernel(rows, streams, *refs):
    n = len(streams)
    ins, outs = refs[:n], refs[n : 2 * n]
    local_sem, recv_sem, z_sem, y_sem, c_sem = refs[2 * n :]
    me, z, y, c = position()
    last = rows - 1
    for i in range(n):
        pltpu.make_async_copy(ins[i], outs[i].at[me], local_sem.at[i]).start()
    greet(rows)
    parts = []
    for i, (width, cut) in enumerate(streams):
        parts.append((i, slice(0, cut), True))
        if cut < width:
            parts.append((i, slice(cut, width), False))

    def copies(k, zz, yy, cc, own):
        i, cols, _ = parts[k]
        block = at(zz, yy, cc)
        src = ins[i].at[:, cols] if own else outs[i].at[block, :, cols]
        dst = outs[i].at[block, :, cols]
        got = recv_sem.at[k, block]
        line = zz * 2 + yy
        return {
            "up": lambda: remote(src, dst, z_sem.at[k, 0, line], got, at(lax.rem(z + 1, rows), y, c)),
            "down": lambda: remote(
                src, dst, z_sem.at[k, 1, line], got, at(lax.rem(z + last, rows), y, c)
            ),
            "y": lambda: remote(src, dst, y_sem.at[k, line], got, at(z, 1 - y, c)),
            "core": lambda: remote(src, dst, c_sem.at[k, line], got, at(z, y, 1 - c)),
        }

    def await_block(k, zz, yy, cc):
        copies(k, zz, yy, cc, False)["core"]().wait_recv()

    def act(verb, k, zz, yy, own, up, down, across):
        made = copies(k, zz, yy, c, own)
        if up:
            pl.when(z < last)(lambda: getattr(made["up"](), verb)())
        if down:
            pl.when(z > 0)(lambda: getattr(made["down"](), verb)())
        if across:
            getattr(made["y"](), verb)()
        getattr(made["core"](), verb)()

    pass_on = functools.partial(act, "start")
    finish = functools.partial(act, "wait_send")

    def walk(action, waiting):
        for k, (_, _, z_first) in enumerate(parts):
            action(k, z, y, True, True, True, True)
        for k, (_, _, z_first) in enumerate(parts):
            if not z_first:
                if waiting:
                    await_block(k, z, 1 - y, c)
                action(k, z, 1 - y, False, True, True, False)
        for step in range(1, rows):
            for k, (_, _, z_first) in enumerate(parts):
                for yy in (y,) if z_first else (y, 1 - y):

                    @pl.when(z - step >= 0)
                    def _():
                        if waiting:
                            await_block(k, z - step, yy, c)
                        action(k, z - step, yy, False, True, False, z_first)

                    @pl.when(z + step < rows)
                    def _():
                        if waiting:
                            await_block(k, z + step, yy, c)
                        action(k, z + step, yy, False, False, True, z_first)

            for k, (_, _, z_first) in enumerate(parts):
                if z_first:

                    def hand(zz):
                        if waiting:
                            await_block(k, zz, 1 - y, c)
                        action(k, zz, 1 - y, False, False, False, False)

                    if step == 1:
                        hand(z)
                    else:
                        pl.when(z - step + 1 >= 0)(lambda: hand(z - step + 1))
                        pl.when(z + step - 1 < rows)(lambda: hand(z + step - 1))
        for k, (_, _, z_first) in enumerate(parts):
            if z_first:
                pl.when(z - last >= 0)(lambda: hand_last(k, z - last, waiting, action))
                pl.when(z + last < rows)(lambda: hand_last(k, z + last, waiting, action))

    def hand_last(k, zz, waiting, action):
        if waiting:
            await_block(k, zz, 1 - y, c)
        action(k, zz, 1 - y, False, False, False, False)

    walk(pass_on, True)
    for k in range(len(parts)):
        for zz in range(rows):
            for yy in range(2):
                await_block(k, zz, yy, 1 - c)
    walk(finish, False)
    for i in range(n):
        pltpu.make_async_copy(ins[i], outs[i].at[me], local_sem.at[i]).wait()


def gather(arrays, cuts, seq, collective_id, name):
    streams = tuple((a.shape[1], cut) for a, cut in zip(arrays, cuts))
    k = sum(1 if cut >= width else 2 for width, cut in streams)
    rows = seq // 4
    dma = pltpu.SemaphoreType.DMA
    return pl.pallas_call(
        functools.partial(gather_kernel, rows, streams),
        out_shape=[jax.ShapeDtypeStruct((seq,) + a.shape, a.dtype) for a in arrays],
        in_specs=[pl.BlockSpec(memory_space=pltpu.VMEM)] * len(arrays),
        out_specs=[pl.BlockSpec(memory_space=pltpu.VMEM)] * len(arrays),
        scratch_shapes=[
            dma((len(arrays),)),
            dma((k, seq)),
            dma((k, 2, 2 * rows)),
            dma((k, 2 * rows)),
            dma((k, 2 * rows)),
        ],
        compiler_params=pltpu.CompilerParams(
            collective_id=collective_id, has_side_effects=True, vmem_limit_bytes=48 * 1024 * 1024
        ),
        cost_estimate=pl.CostEstimate(flops=0, bytes_accessed=100_000_000, transcendentals=0),
        name=name,
    )(*arrays)


def scatter_kernel(
    rows, part_ref, res_ref, gain_ref, out_ref, acc, c_buf, ya_buf, za_buf, zb_buf, yb_buf, mix,
    cs, cr, yas, yar, zas, zar, zbs, zbr, ybs, ybr,
):
    me, z, y, c = position()
    last = rows - 1
    half = part_ref.shape[2] // 2
    left, right = slice(0, half), slice(half, 2 * half)
    above, below = lax.rem(z + 1, rows), lax.rem(z + last, rows)
    other_y, other_c = at(z, 1 - y, c), at(z, y, 1 - c)
    greet(rows)
    order = []
    for i in range((rows + 1) // 2):
        order += [i] if i == last - i else [i, last - i]

    def core_copy(zz, yy):
        line = zz * 2 + yy
        return remote(part_ref.at[at(zz, yy, 1 - c)], c_buf.at[line], cs.at[line], cr.at[line], other_c)

    def ya_copy(zz):
        return remote(acc.at[zz * 2 + 1 - y, :, left], ya_buf.at[zz], yas.at[zz], yar.at[zz], other_y)

    def yb_copy():
        return remote(acc.at[z * 2 + 1 - y, :, right], yb_buf, ybs, ybr, other_y)

    def za_copy(zz, way):
        target = at(above if way == 0 else below, y, c)
        return remote(acc.at[zz * 2 + y, :, left], za_buf.at[way, zz], zas.at[zz], zar.at[way, zz], target)

    def zb_copy(zz, yy, way):
        target = at(above if way == 0 else below, y, c)
        line = zz * 2 + yy
        return remote(acc.at[line, :, right], zb_buf.at[way, line], zbs.at[line], zbr.at[way, line], target)

    def add(line, cols, value):
        acc[line, :, cols] = (acc[line, :, cols].astype(F32) + value.astype(F32)).astype(BF16)

    for zz in order:
        for yy in (1 - y, y):
            core_copy(zz, yy).start()
    for zz in order:
        for yy in (1 - y, y):
            line = zz * 2 + yy
            core_copy(zz, yy).wait_recv()
            acc[line] = (part_ref[at(zz, yy, c)].astype(F32) + c_buf[line].astype(F32)).astype(BF16)
            if zz < last:
                pl.when(z == last)(lambda: zb_copy(zz, yy, 1).start())
            if zz > 0:
                pl.when(z == 0)(lambda: zb_copy(zz, yy, 0).start())
        ya_copy(zz).start()
    for zz in order:

        def add_za(way):
            za_copy(zz, way).wait_recv()
            add(zz * 2 + y, left, za_buf[way, zz])

        def add_zb(yy, way):
            zb_copy(zz, yy, way).wait_recv()
            add(zz * 2 + yy, right, zb_buf[way, zz * 2 + yy])

        for yy in (1 - y, y):

            @pl.when((z > zz) & (z < last))
            def _():
                add_zb(yy, 1)
                zb_copy(zz, yy, 1).start()

            @pl.when((z < zz) & (z > 0))
            def _():
                add_zb(yy, 0)
                zb_copy(zz, yy, 0).start()

        ya_copy(zz).wait_recv()
        add(zz * 2 + y, left, ya_buf[zz])

        @pl.when(z > zz)
        def _():
            pl.when(z < last)(lambda: add_za(1))
            za_copy(zz, 1).start()

        @pl.when(z < zz)
        def _():
            pl.when(z > 0)(lambda: add_za(0))
            za_copy(zz, 0).start()

    for yy in (1 - y, y):
        line = z * 2 + yy

        @pl.when(z < last)
        def _():
            zb_copy(z, yy, 1).wait_recv()
            add(line, right, zb_buf[1, line])

        @pl.when(z > 0)
        def _():
            zb_copy(z, yy, 0).wait_recv()
            add(line, right, zb_buf[0, line])

    yb_copy().start()
    mine = z * 2 + y
    mix[:, left] = res_ref[:, left].astype(F32) + acc[mine, :, left].astype(F32)

    @pl.when(z < last)
    def _():
        za_copy(z, 1).wait_recv()
        mix[:, left] += za_buf[1, z].astype(F32)

    @pl.when(z > 0)
    def _():
        za_copy(z, 0).wait_recv()
        mix[:, left] += za_buf[0, z].astype(F32)

    yb_copy().wait_recv()
    mix[:, right] = res_ref[:, right].astype(F32) + (
        acc[mine, :, right].astype(F32) + yb_buf[...].astype(F32)
    )
    mixed = mix[...]
    scale = lax.rsqrt(jnp.mean(mixed * mixed, axis=-1, keepdims=True) + 1e-05)
    out_ref[...] = (mixed * scale * gain_ref[...]).astype(BF16)
    for zz in range(rows):
        for yy in range(2):
            core_copy(zz, yy).wait_send()
            pl.when(z > zz)(lambda: zb_copy(zz, yy, 1).wait_send())
            pl.when(z < zz)(lambda: zb_copy(zz, yy, 0).wait_send())
        ya_copy(zz).wait_send()
        pl.when(z > zz)(lambda: za_copy(zz, 1).wait_send())
        pl.when(z < zz)(lambda: za_copy(zz, 0).wait_send())
    yb_copy().wait_send()


def scatter_norm(partial, residual, gain, seq):
    _, tokens, width = partial.shape
    rows = seq // 4
    half = width // 2
    dma = pltpu.SemaphoreType.DMA
    return pl.pallas_call(
        functools.partial(scatter_kernel, rows),
        out_shape=jax.ShapeDtypeStruct((tokens, width), BF16),
        in_specs=[pl.BlockSpec(memory_space=pltpu.VMEM)] * 3,
        out_specs=pl.BlockSpec(memory_space=pltpu.VMEM),
        scratch_shapes=[
            pltpu.VMEM((2 * rows, tokens, width), BF16),
            pltpu.VMEM((2 * rows, tokens, width), BF16),
            pltpu.VMEM((rows, tokens, half), BF16),
            pltpu.VMEM((2, rows, tokens, half), BF16),
            pltpu.VMEM((2, 2 * rows, tokens, half), BF16),
            pltpu.VMEM((tokens, half), BF16),
            pltpu.VMEM((tokens, width), F32),
            dma((2 * rows,)),
            dma((2 * rows,)),
            dma((rows,)),
            dma((rows,)),
            dma((rows,)),
            dma((2, rows)),
            dma((2 * rows,)),
            dma((2, 2 * rows)),
            dma,
            dma,
        ],
        compiler_params=pltpu.CompilerParams(
            collective_id=2, has_side_effects=True, vmem_limit_bytes=48 * 1024 * 1024
        ),
        cost_estimate=pl.CostEstimate(flops=0, bytes_accessed=100_000_000, transcendentals=0),
        name="scatter_norm",
    )(partial, residual, gain.reshape(1, width))


def on_device(
    moe_input,
    residual_in,
    expert_ids,
    route_logits,
    kept_blocks,
    w_gate,
    w_up,
    w_down,
    norm_gain,
    qkv_weight,
):
    tokens, width = moe_input.shape
    seq = lax.axis_size("seq")
    me = lax.axis_index("seq")
    cap = min(tokens, max(2, tokens * TOP * 2 // seq))
    raised = jnp.exp(route_logits)
    weights = raised / jnp.sum(raised, axis=-1, keepdims=True)
    meta = jnp.concatenate([expert_ids.astype(F32), weights], axis=1).T
    qkv_full = lax.all_gather(qkv_weight, "seq", axis=0, tiled=True)
    rows, meta = gather((moe_input, meta), (width // 2, tokens), seq, 0, "gather_tokens")

    hit = (meta[:, :TOP] == me.astype(F32)).astype(F32)
    share = jnp.sum(hit * meta[:, TOP:], axis=1)
    named = jnp.sum(hit, axis=1)
    earlier = (jnp.arange(tokens)[:, None] < jnp.arange(tokens)[None, :]).astype(F32)
    slot = jnp.dot(named, earlier)
    slot = jnp.where(named > 0.5, slot, -1.0)
    place = (slot[:, None, :] == jnp.arange(cap, dtype=F32)[None, :, None]).astype(BF16)
    sent = jnp.einsum(
        "sct,std->scd", place, rows, preferred_element_type=F32
    ).astype(BF16).reshape(seq * cap, width)
    gate_part = jnp.dot(sent, w_gate[0], preferred_element_type=F32)
    up_part = jnp.dot(sent, w_up[0], preferred_element_type=F32)
    hidden = jax.nn.silu(gate_part) * up_part
    energy = jnp.sqrt(jnp.sum(hidden * hidden, axis=0) / (seq * cap) + 1e-06)
    result = jnp.dot(hidden.astype(BF16), w_down[0], preferred_element_type=F32).astype(BF16)
    chosen = (kept_blocks[0][:, None] == jnp.arange(OB, dtype=jnp.int32)[None, :]).astype(F32)
    placed = jnp.einsum(
        "bo,bc->oc", chosen, energy.reshape(KB, BLOCK), precision=lax.Precision.HIGHEST
    )
    neuron_energy = placed.reshape(1, OB * BLOCK)
    back = jnp.einsum(
        "sct,scd->std", place, result.reshape(seq, cap, width), preferred_element_type=F32
    )
    partial = (back * share[..., None]).astype(BF16)
    if seq <= 16:
        normed = scatter_norm(partial, residual_in, norm_gain, seq)
    else:
        moe = lax.psum_scatter(
            partial.reshape(seq * tokens, width), "seq", scatter_dimension=0, tiled=True
        )
        mixed = residual_in.astype(F32) + moe.astype(F32)
        normed = (
            mixed * lax.rsqrt(jnp.mean(mixed * mixed, axis=-1, keepdims=True) + 1e-05) * norm_gain
        ).astype(BF16)
    query_width = QH * HD
    keys_vals = jnp.dot(normed, qkv_full[:, query_width:], preferred_element_type=F32).astype(BF16)
    (kv,) = gather((keys_vals,), (KVH * HD,), seq, 1, "gather_kv")
    kv = kv.reshape(seq * tokens, 2 * KVH * HD)
    queries = jnp.dot(normed, qkv_full[:, :query_width], preferred_element_type=F32).astype(BF16)
    attention = attention_call((queries * HD ** (-0.5)).T, kv)
    return (attention, neuron_energy)


def solution(mesh):
    return jax.shard_map(
        on_device,
        mesh=mesh,
        in_specs=(
            P(("groups", "seq"), None),
            P(("groups", "seq"), None),
            P(("groups", "seq"), None),
            P(("groups", "seq"), None),
            P("seq", None),
            P("seq", None, None),
            P("seq", None, None),
            P("seq", None, None),
            P(),
            P("seq", None),
        ),
        out_specs=(P(("groups", "seq"), None), P("seq", "groups")),
        check_vma=False,
    )
```

```python
import functools

import jax
import jax.numpy as jnp
from jax import lax
from jax.experimental import pallas as pl
from jax.experimental.pallas import tpu as pltpu
from jax.sharding import PartitionSpec as P

TOP = 4
BLOCK = 128
KB = 6
OB = 12
QH = 32
KVH = 4
HD = 64
BK = 256
QCHUNK = 512
F32 = jnp.float32
BF16 = jnp.bfloat16


def attention_kernel(qt_ref, kv_ref, out_ref, q_scr, m_scr, l_scr, acc_scr):
    me = lax.axis_index("seq")
    tokens = qt_ref.shape[1]
    heads = QCHUNK // tokens
    chunks = QH // heads
    for c in range(chunks):
        for h in range(heads):
            row = (c * heads + h) * HD
            q_scr[c, :, h * tokens : (h + 1) * tokens] = qt_ref[row : row + HD, :]
    m_scr[...] = jnp.full_like(m_scr, -1e30)
    l_scr[...] = jnp.zeros_like(l_scr)
    acc_scr[...] = jnp.zeros_like(acc_scr)

    def block(kb, masked):
        start = pl.multiple_of(kb * BK, BK)
        if masked:
            key_pos = start + lax.broadcasted_iota(jnp.int32, (BK, tokens), 0)
            query_pos = me * tokens + lax.broadcasted_iota(jnp.int32, (BK, tokens), 1)
            hide = jnp.where(key_pos <= query_pos, 0.0, -1e30)
            hide = jnp.concatenate([hide] * heads, axis=1)
        for c in range(chunks):
            g = c * heads // (QH // KVH)
            keys = kv_ref[pl.ds(start, BK), g * HD : (g + 1) * HD]
            vals = kv_ref[pl.ds(start, BK), (KVH + g) * HD : (KVH + g + 1) * HD]
            s = jnp.dot(keys, q_scr[c], preferred_element_type=F32)
            if masked:
                s = s + hide
            m_old = m_scr[c]
            m_new = jnp.maximum(m_old, jnp.max(s, axis=0, keepdims=True))
            p = jnp.exp(s - m_new)
            alpha = jnp.exp(m_old - m_new)
            m_scr[c] = m_new
            l_scr[c] = l_scr[c] * alpha + jnp.sum(p, axis=0, keepdims=True)
            pv = lax.dot_general(
                vals, p.astype(BF16), (((0,), (0,)), ((), ())), preferred_element_type=F32
            )
            acc_scr[c] = acc_scr[c] * alpha + pv

    full = me * tokens // BK

    @pl.loop(0, full)
    def _(kb):
        block(kb, False)

    block(full, True)
    for c in range(chunks):
        o = acc_scr[c] / l_scr[c]
        for h in range(0, heads, 2):
            pair = jnp.concatenate(
                [o[:, h * tokens : (h + 1) * tokens], o[:, (h + 1) * tokens : (h + 2) * tokens]], axis=0
            )
            col = (c * heads + h) * HD
            out_ref[:, col : col + 2 * HD] = pair.T.astype(BF16)


def attention_call(qt, kv):
    tokens = qt.shape[1]
    chunks = QH * tokens // QCHUNK
    return pl.pallas_call(
        attention_kernel,
        out_shape=jax.ShapeDtypeStruct((tokens, QH * HD), BF16),
        in_specs=[pl.BlockSpec(memory_space=pltpu.VMEM)] * 2,
        out_specs=pl.BlockSpec(memory_space=pltpu.VMEM),
        scratch_shapes=[
            pltpu.VMEM((chunks, HD, QCHUNK), BF16),
            pltpu.VMEM((chunks, 1, QCHUNK), F32),
            pltpu.VMEM((chunks, 1, QCHUNK), F32),
            pltpu.VMEM((chunks, HD, QCHUNK), F32),
        ],
        compiler_params=pltpu.CompilerParams(vmem_limit_bytes=40 * 1024 * 1024),
        name="attention",
    )(qt, kv)


MESH = pl.DeviceIdType.MESH


def position():
    me = lax.axis_index("seq")
    return me, me // 4, (me // 2) % 2, me % 2


def at(z, y, c):
    return (z * 2 + y) * 2 + c


def remote(src, dst, send_sem, recv_sem, target):
    return pltpu.make_async_remote_copy(
        src_ref=src,
        dst_ref=dst,
        send_sem=send_sem,
        recv_sem=recv_sem,
        device_id={"seq": target},
        device_id_type=MESH,
    )


def greet(rows):
    me, z, y, c = position()
    barrier = pltpu.get_barrier_semaphore()
    near = (
        at((z + 1) % rows, y, c),
        at((z + rows - 1) % rows, y, c),
        at(z, 1 - y, c),
        at(z, y, 1 - c),
    )
    for target in near:
        pl.semaphore_signal(barrier, inc=1, device_id={"seq": target}, device_id_type=MESH)
    pl.semaphore_wait(barrier, len(near))


def experts_kernel(
    rows, cap, x_ref, meta_ref, wq_ref, wg_ref, wu_ref, wd_ref,
    part_ref, energy_ref, wq_out, x_all, meta_all, sent, place_scr, local_sem, recv_sem, z_sem, y_sem, c_sem,
):
    me, z, y, c = position()
    last = rows - 1
    tokens, width = x_ref.shape
    half, whalf = width // 2, wq_ref.shape[1] // 2
    ins, outs = (x_ref, meta_ref, wq_ref), (x_all, meta_all, wq_out)
    parts = (
        (0, slice(0, half), True),
        (0, slice(half, width), False),
        (1, slice(0, tokens), True),
        (2, slice(0, whalf), True),
        (2, slice(whalf, 2 * whalf), False),
    )

    def own_copy(i):
        return pltpu.make_async_copy(ins[i], outs[i].at[me], local_sem.at[i])

    for i in range(3):
        own_copy(i).start()
    greet(rows)

    def copies(k, zz, yy, cc, own):
        i, cols, _ = parts[k]
        block = at(zz, yy, cc)
        src = ins[i].at[:, cols] if own else outs[i].at[block, :, cols]
        dst = outs[i].at[block, :, cols]
        got = recv_sem.at[k, block]
        line = zz * 2 + yy
        return {
            "up": lambda: remote(src, dst, z_sem.at[k, 0, line], got, at(lax.rem(z + 1, rows), y, c)),
            "down": lambda: remote(
                src, dst, z_sem.at[k, 1, line], got, at(lax.rem(z + last, rows), y, c)
            ),
            "y": lambda: remote(src, dst, y_sem.at[k, line], got, at(z, 1 - y, c)),
            "core": lambda: remote(src, dst, c_sem.at[k, line], got, at(z, y, 1 - c)),
        }

    def await_block(k, zz, yy, cc):
        copies(k, zz, yy, cc, False)["core"]().wait_recv()

    def act(verb, k, zz, yy, own, up, down, across):
        made = copies(k, zz, yy, c, own)
        if up:
            pl.when(z < last)(lambda: getattr(made["up"](), verb)())
        if down:
            pl.when(z > 0)(lambda: getattr(made["down"](), verb)())
        if across:
            getattr(made["y"](), verb)()
        getattr(made["core"](), verb)()

    def pass_on(*args):
        act("start", *args)

    def finish(*args):
        act("wait_send", *args)

    def walk_step(chosen, step, action, waiting):
        def reached(k, zz, yy, up, down, across):
            if waiting:
                await_block(k, zz, yy, c)
            action(k, zz, yy, False, up, down, across)

        if step == 0:
            for k in chosen:
                action(k, z, y, True, True, True, True)
            return
        if step == 1:
            for k in chosen:
                if not parts[k][2]:
                    reached(k, z, 1 - y, True, True, False)
        if step < rows:
            for k in chosen:
                z_first = parts[k][2]
                for yy in (y,) if z_first else (y, 1 - y):

                    @pl.when(z - step >= 0)
                    def _():
                        reached(k, z - step, yy, True, False, z_first)

                    @pl.when(z + step < rows)
                    def _():
                        reached(k, z + step, yy, False, True, z_first)

        for k in chosen:
            if parts[k][2]:
                if step == 1:
                    reached(k, z, 1 - y, False, False, False)
                else:

                    @pl.when(z - step + 1 >= 0)
                    def _():
                        reached(k, z - step + 1, 1 - y, False, False, False)

                    @pl.when(z + step - 1 < rows)
                    def _():
                        reached(k, z + step - 1, 1 - y, False, False, False)

    def from_core(chosen):
        for k in chosen:
            for zz in range(rows):
                for yy in range(2):
                    await_block(k, zz, yy, 1 - c)

    first, second = (2, 0, 1), (3, 4)
    for step in range(rows + 1):
        walk_step(first, step, pass_on, True)
    walk_step(second, 0, pass_on, True)
    from_core(first)
    own_copy(0).wait()
    own_copy(1).wait()

    batch = 2 * 2
    earlier = (
        lax.broadcasted_iota(jnp.int32, (tokens, tokens), 0)
        < lax.broadcasted_iota(jnp.int32, (tokens, tokens), 1)
    ).astype(F32).astype(BF16)
    slots = lax.broadcasted_iota(jnp.int32, (cap, tokens), 0).astype(F32)
    mine = me.astype(F32)
    energy_ref[...] = jnp.zeros_like(energy_ref)
    for b in range(rows):
        shares = []
        for i in range(batch):
            block = b * batch + i
            meta = meta_all[block]
            hit = jnp.where(meta[:TOP] == mine, 1.0, 0.0)
            named = jnp.sum(hit, axis=0, keepdims=True)
            shares.append(jnp.sum(hit * meta[TOP:], axis=0, keepdims=True))
            slot = jnp.dot(
                jnp.broadcast_to(named, (16, tokens)).astype(BF16), earlier, preferred_element_type=F32
            )[:1]
            slot = jnp.where(named > 0.5, slot, -1.0)
            place = jnp.where(slots == slot, 1.0, 0.0).astype(BF16)
            place_scr[i] = place
            sent[i * cap : (i + 1) * cap, :] = jnp.dot(
                place, x_all[block], preferred_element_type=F32
            ).astype(BF16)
        gate_part = jnp.dot(sent[...], wg_ref[...], preferred_element_type=F32)
        up_part = jnp.dot(sent[...], wu_ref[...], preferred_element_type=F32)
        hidden = gate_part / (1.0 + jnp.exp(-gate_part)) * up_part
        energy_ref[...] += jnp.sum(hidden * hidden, axis=0, keepdims=True)
        result = jnp.dot(hidden.astype(BF16), wd_ref[...], preferred_element_type=F32).astype(BF16)
        for i in range(batch):
            back = lax.dot_general(
                place_scr[i],
                result[i * cap : (i + 1) * cap],
                (((0,), (0,)), ((), ())),
                preferred_element_type=F32,
            )
            share = jnp.broadcast_to(shares[i], (tokens, tokens)).T[:, :1]
            part_ref[b * batch + i] = (back * share).astype(BF16)
        walk_step(second, b + 1, pass_on, True)
    from_core(second)
    for step in range(rows + 1):
        walk_step(first + second, step, finish, False)
    own_copy(2).wait()


def experts(x, meta, wq, wg, wu, wd, seq, cap):
    tokens, width = x.shape
    rows = seq // 4
    dma = pltpu.SemaphoreType.DMA
    return pl.pallas_call(
        functools.partial(experts_kernel, rows, cap),
        out_shape=[
            jax.ShapeDtypeStruct((seq, tokens, width), BF16),
            jax.ShapeDtypeStruct((1, wg.shape[1]), F32),
            jax.ShapeDtypeStruct((seq,) + wq.shape, BF16),
        ],
        in_specs=[pl.BlockSpec(memory_space=pltpu.VMEM)] * 6,
        out_specs=[pl.BlockSpec(memory_space=pltpu.VMEM)] * 3,
        scratch_shapes=[
            pltpu.VMEM((seq, tokens, width), BF16),
            pltpu.VMEM((seq, 2 * TOP, tokens), F32),
            pltpu.VMEM((4 * cap, width), BF16),
            pltpu.VMEM((4, cap, tokens), BF16),
            dma((3,)),
            dma((5, seq)),
            dma((5, 2, 2 * rows)),
            dma((5, 2 * rows)),
            dma((5, 2 * rows)),
        ],
        compiler_params=pltpu.CompilerParams(
            collective_id=0, has_side_effects=True, vmem_limit_bytes=56 * 1024 * 1024
        ),
        name="experts",
    )(x, meta, wq, wg, wu, wd)


def scatter_kernel(
    rows, part_ref, res_ref, gain_ref, out_ref, acc, c_buf, ya_buf, za_buf, zb_buf, yb_buf, mix,
    cs, cr, yas, yar, zas, zar, zbs, zbr, ybs, ybr,
):
    me, z, y, c = position()
    last = rows - 1
    half = part_ref.shape[2] // 2
    left, right = slice(0, half), slice(half, 2 * half)
    above, below = lax.rem(z + 1, rows), lax.rem(z + last, rows)
    other_y, other_c = at(z, 1 - y, c), at(z, y, 1 - c)
    greet(rows)
    order = []
    for i in range((rows + 1) // 2):
        order += [i] if i == last - i else [i, last - i]

    def core_copy(zz, yy):
        line = zz * 2 + yy
        return remote(part_ref.at[at(zz, yy, 1 - c)], c_buf.at[line], cs.at[line], cr.at[line], other_c)

    def ya_copy(zz):
        return remote(acc.at[zz * 2 + 1 - y, :, left], ya_buf.at[zz], yas.at[zz], yar.at[zz], other_y)

    def yb_copy():
        return remote(acc.at[z * 2 + 1 - y, :, right], yb_buf, ybs, ybr, other_y)

    def za_copy(zz, way):
        target = at(above if way == 0 else below, y, c)
        return remote(acc.at[zz * 2 + y, :, left], za_buf.at[way, zz], zas.at[zz], zar.at[way, zz], target)

    def zb_copy(zz, yy, way):
        target = at(above if way == 0 else below, y, c)
        line = zz * 2 + yy
        return remote(acc.at[line, :, right], zb_buf.at[way, line], zbs.at[line], zbr.at[way, line], target)

    def add(line, cols, value):
        acc[line, :, cols] = (acc[line, :, cols].astype(F32) + value.astype(F32)).astype(BF16)

    for zz in order:
        for yy in (1 - y, y):
            core_copy(zz, yy).start()
    for zz in order:
        for yy in (1 - y, y):
            line = zz * 2 + yy
            core_copy(zz, yy).wait_recv()
            acc[line] = (part_ref[at(zz, yy, c)].astype(F32) + c_buf[line].astype(F32)).astype(BF16)
            if zz < last:
                pl.when(z == last)(lambda: zb_copy(zz, yy, 1).start())
            if zz > 0:
                pl.when(z == 0)(lambda: zb_copy(zz, yy, 0).start())
        ya_copy(zz).start()
    for zz in order:

        def add_za(way):
            za_copy(zz, way).wait_recv()
            add(zz * 2 + y, left, za_buf[way, zz])

        def add_zb(yy, way):
            zb_copy(zz, yy, way).wait_recv()
            add(zz * 2 + yy, right, zb_buf[way, zz * 2 + yy])

        for yy in (1 - y, y):

            @pl.when((z > zz) & (z < last))
            def _():
                add_zb(yy, 1)
                zb_copy(zz, yy, 1).start()

            @pl.when((z < zz) & (z > 0))
            def _():
                add_zb(yy, 0)
                zb_copy(zz, yy, 0).start()

        ya_copy(zz).wait_recv()
        add(zz * 2 + y, left, ya_buf[zz])

        @pl.when(z > zz)
        def _():
            pl.when(z < last)(lambda: add_za(1))
            za_copy(zz, 1).start()

        @pl.when(z < zz)
        def _():
            pl.when(z > 0)(lambda: add_za(0))
            za_copy(zz, 0).start()

    for yy in (1 - y, y):
        line = z * 2 + yy

        @pl.when(z < last)
        def _():
            zb_copy(z, yy, 1).wait_recv()
            add(line, right, zb_buf[1, line])

        @pl.when(z > 0)
        def _():
            zb_copy(z, yy, 0).wait_recv()
            add(line, right, zb_buf[0, line])

    yb_copy().start()
    mine = z * 2 + y
    mix[:, left] = res_ref[:, left].astype(F32) + acc[mine, :, left].astype(F32)

    @pl.when(z < last)
    def _():
        za_copy(z, 1).wait_recv()
        mix[:, left] += za_buf[1, z].astype(F32)

    @pl.when(z > 0)
    def _():
        za_copy(z, 0).wait_recv()
        mix[:, left] += za_buf[0, z].astype(F32)

    yb_copy().wait_recv()
    mix[:, right] = res_ref[:, right].astype(F32) + (
        acc[mine, :, right].astype(F32) + yb_buf[...].astype(F32)
    )
    mixed = mix[...]
    scale = lax.rsqrt(jnp.mean(mixed * mixed, axis=-1, keepdims=True) + 1e-05)
    out_ref[...] = (mixed * scale * gain_ref[...]).astype(BF16)
    for zz in range(rows):
        for yy in range(2):
            core_copy(zz, yy).wait_send()
            pl.when(z > zz)(lambda: zb_copy(zz, yy, 1).wait_send())
            pl.when(z < zz)(lambda: zb_copy(zz, yy, 0).wait_send())
        ya_copy(zz).wait_send()
        pl.when(z > zz)(lambda: za_copy(zz, 1).wait_send())
        pl.when(z < zz)(lambda: za_copy(zz, 0).wait_send())
    yb_copy().wait_send()


def scatter_norm(partial, residual, gain, seq):
    _, tokens, width = partial.shape
    rows = seq // 4
    half = width // 2
    dma = pltpu.SemaphoreType.DMA
    return pl.pallas_call(
        functools.partial(scatter_kernel, rows),
        out_shape=jax.ShapeDtypeStruct((tokens, width), BF16),
        in_specs=[pl.BlockSpec(memory_space=pltpu.VMEM)] * 3,
        out_specs=pl.BlockSpec(memory_space=pltpu.VMEM),
        scratch_shapes=[
            pltpu.VMEM((2 * rows, tokens, width), BF16),
            pltpu.VMEM((2 * rows, tokens, width), BF16),
            pltpu.VMEM((rows, tokens, half), BF16),
            pltpu.VMEM((2, rows, tokens, half), BF16),
            pltpu.VMEM((2, 2 * rows, tokens, half), BF16),
            pltpu.VMEM((tokens, half), BF16),
            pltpu.VMEM((tokens, width), F32),
            dma((2 * rows,)),
            dma((2 * rows,)),
            dma((rows,)),
            dma((rows,)),
            dma((rows,)),
            dma((2, rows)),
            dma((2 * rows,)),
            dma((2, 2 * rows)),
            dma,
            dma,
        ],
        compiler_params=pltpu.CompilerParams(
            collective_id=2, has_side_effects=True, vmem_limit_bytes=48 * 1024 * 1024
        ),
        cost_estimate=pl.CostEstimate(flops=0, bytes_accessed=100_000_000, transcendentals=0),
        name="scatter_norm",
    )(partial, residual, gain.reshape(1, width))


def qkv_attention_kernel(
    rows, n_ref, w_ref, out_ref, kv_own, kv_all, q_scr, m_scr, l_scr, acc_scr, recv_sem, z_sem, y_sem, c_sem
):
    me, z, y, c = position()
    last = rows - 1
    tokens = n_ref.shape[0]
    query_width = QH * HD
    heads = QCHUNK // tokens
    chunks = QH // heads
    greet(rows)
    normed = n_ref[...]
    kv_own[...] = jnp.dot(normed, w_ref[:, query_width:], preferred_element_type=F32).astype(BF16)

    def place(zz, yy, cc):
        return kv_all.at[zz * 2 + yy, pl.ds(pl.multiple_of(cc * tokens, tokens), tokens), :]

    def copies(zz, yy, own):
        src = kv_own if own else place(zz, yy, c)
        dst = place(zz, yy, c)
        line = zz * 2 + yy
        got = recv_sem.at[at(zz, yy, c)]
        return {
            "up": lambda: remote(src, dst, z_sem.at[line], got, at(lax.rem(z + 1, rows), y, c)),
            "y": lambda: remote(src, dst, y_sem.at[line], got, at(z, 1 - y, c)),
            "core": lambda: remote(src, dst, c_sem.at[line], got, at(z, y, 1 - c)),
        }

    def await_block(zz, yy, cc):
        dst = place(zz, yy, cc)
        remote(dst, dst, c_sem.at[0], recv_sem.at[at(zz, yy, cc)], at(z, y, 1 - c)).wait_recv()

    def act(verb, zz, yy, own, along):
        made = copies(zz, yy, own)
        if along:
            pl.when(z < last)(lambda: getattr(made["up"](), verb)())
            getattr(made["y"](), verb)()
        getattr(made["core"](), verb)()

    act("start", z, y, True, True)
    kv_all[z * 2 + y, pl.ds(pl.multiple_of(c * tokens, tokens), tokens), :] = kv_own[...]
    m_scr[...] = jnp.full_like(m_scr, -1e30)
    l_scr[...] = jnp.zeros_like(l_scr)
    acc_scr[...] = jnp.zeros_like(acc_scr)
    step_cols = QCHUNK // tokens * HD
    for ch in range(chunks):
        q = jnp.dot(
            normed, w_ref[:, ch * step_cols : (ch + 1) * step_cols], preferred_element_type=F32
        )
        q = q.astype(BF16).astype(F32) * HD ** (-0.5)
        for h in range(0, heads, 2):
            pair = q[:, h * HD : (h + 2) * HD].T.astype(BF16)
            q_scr[ch, :, h * tokens : (h + 1) * tokens] = pair[:HD]
            q_scr[ch, :, (h + 1) * tokens : (h + 2) * tokens] = pair[HD:]

    def block(line, masked):
        if masked:
            key_pos = lax.broadcasted_iota(jnp.int32, (BK, tokens), 0)
            query_pos = c * tokens + lax.broadcasted_iota(jnp.int32, (BK, tokens), 1)
            hide = jnp.where(key_pos <= query_pos, 0.0, -1e30)
            hide = jnp.concatenate([hide] * heads, axis=1)
        for ch in range(chunks):
            g = ch * heads // (QH // KVH)
            keys = kv_all[line, :, g * HD : (g + 1) * HD]
            vals = kv_all[line, :, (KVH + g) * HD : (KVH + g + 1) * HD]
            s = jnp.dot(keys, q_scr[ch], preferred_element_type=F32)
            if masked:
                s = s + hide
            m_old = m_scr[ch]
            m_new = jnp.maximum(m_old, jnp.max(s, axis=0, keepdims=True))
            p = jnp.exp(s - m_new)
            alpha = jnp.exp(m_old - m_new)
            m_scr[ch] = m_new
            l_scr[ch] = l_scr[ch] * alpha + jnp.sum(p, axis=0, keepdims=True)
            pv = lax.dot_general(
                vals, p.astype(BF16), (((0,), (0,)), ((), ())), preferred_element_type=F32
            )
            acc_scr[ch] = acc_scr[ch] * alpha + pv

    def relay(zz, yy, along):
        await_block(zz, yy, c)
        act("start", zz, yy, False, along)

    relay(z, 1 - y, False)
    pl.when(z >= 1)(lambda: relay(z - 1, y, True))
    await_block(z, y, 1 - c)
    block(z * 2 + y, True)
    for step in range(1, rows + 1):
        if step < last:
            pl.when(z >= step + 1)(lambda: relay(z - step - 1, y, True))
        if step <= last:
            pl.when(z >= step)(lambda: relay(z - step, 1 - y, False))
        back = step - 1

        @pl.when(z >= back)
        def _():
            await_block(z - back, 1 - y, 1 - c)
            if back > 0:
                await_block(z - back, y, 1 - c)

        if back == 0:
            pl.when(y == 1)(lambda: block(z * 2, False))
        else:

            @pl.when(z >= back)
            def _():
                @pl.loop(0, 2)
                def _(yy):
                    block((z - back) * 2 + yy, False)

    for ch in range(chunks):
        o = acc_scr[ch] / l_scr[ch]
        for h in range(0, heads, 2):
            pair = jnp.concatenate(
                [o[:, h * tokens : (h + 1) * tokens], o[:, (h + 1) * tokens : (h + 2) * tokens]], axis=0
            )
            col = (ch * heads + h) * HD
            out_ref[:, col : col + 2 * HD] = pair.T.astype(BF16)
    act("wait_send", z, y, True, True)
    act("wait_send", z, 1 - y, False, False)
    for back in range(1, rows):
        pl.when(z >= back)(lambda: act("wait_send", z - back, y, False, True))
        pl.when(z >= back)(lambda: act("wait_send", z - back, 1 - y, False, False))


def qkv_attention(normed, weight, seq):
    tokens = normed.shape[0]
    chunks = QH * tokens // QCHUNK
    rows = seq // 4
    dma = pltpu.SemaphoreType.DMA
    return pl.pallas_call(
        functools.partial(qkv_attention_kernel, rows),
        out_shape=jax.ShapeDtypeStruct((tokens, QH * HD), BF16),
        in_specs=[pl.BlockSpec(memory_space=pltpu.VMEM)] * 2,
        out_specs=pl.BlockSpec(memory_space=pltpu.VMEM),
        scratch_shapes=[
            pltpu.VMEM((tokens, 2 * KVH * HD), BF16),
            pltpu.VMEM((2 * rows, 2 * tokens, 2 * KVH * HD), BF16),
            pltpu.VMEM((chunks, HD, QCHUNK), BF16),
            pltpu.VMEM((chunks, 1, QCHUNK), F32),
            pltpu.VMEM((chunks, 1, QCHUNK), F32),
            pltpu.VMEM((chunks, HD, QCHUNK), F32),
            dma((seq,)),
            dma((2 * rows,)),
            dma((2 * rows,)),
            dma((2 * rows,)),
        ],
        compiler_params=pltpu.CompilerParams(
            collective_id=1, has_side_effects=True, vmem_limit_bytes=48 * 1024 * 1024
        ),
        name="qkv_attention",
    )(normed, weight)


def on_device(
    moe_input,
    residual_in,
    expert_ids,
    route_logits,
    kept_blocks,
    w_gate,
    w_up,
    w_down,
    norm_gain,
    qkv_weight,
):
    tokens, width = moe_input.shape
    seq = lax.axis_size("seq")
    me = lax.axis_index("seq")
    cap = min(tokens, max(2, tokens * TOP * 2 // seq))
    raised = jnp.exp(route_logits)
    weights = raised / jnp.sum(raised, axis=-1, keepdims=True)
    chosen = (kept_blocks[0][:, None] == jnp.arange(OB, dtype=jnp.int32)[None, :]).astype(F32)

    def unpruned(squares):
        energy = jnp.sqrt(squares / (seq * cap) + 1e-06)
        placed = jnp.einsum(
            "bo,bc->oc", chosen, energy.reshape(KB, BLOCK), precision=lax.Precision.HIGHEST
        )
        return placed.reshape(1, OB * BLOCK)

    meta = jnp.concatenate([expert_ids.astype(F32), weights], axis=1)
    if seq == 16 and tokens == 128:
        partial, squares, qkv_full = experts(
            moe_input, meta.T, qkv_weight, w_gate[0], w_up[0], w_down[0], seq, cap
        )
        normed = scatter_norm(partial, residual_in, norm_gain, seq)
        attention = qkv_attention(normed, qkv_full.reshape(width, -1), seq)
        return (attention, unpruned(squares))
    meta = lax.all_gather(meta, "seq", axis=0, tiled=True)
    rows = lax.all_gather(moe_input, "seq", axis=0, tiled=True)
    qkv_full = lax.all_gather(qkv_weight, "seq", axis=0, tiled=True)

    hit = (meta[:, :TOP] == me.astype(F32)).astype(F32)
    share = jnp.sum(hit * meta[:, TOP:], axis=1).reshape(seq, tokens)
    named = jnp.sum(hit, axis=1).reshape(seq, tokens)
    earlier = (jnp.arange(tokens)[:, None] < jnp.arange(tokens)[None, :]).astype(F32)
    slot = jnp.dot(named, earlier)
    slot = jnp.where(named > 0.5, slot, -1.0)
    place = (slot[:, None, :] == jnp.arange(cap, dtype=F32)[None, :, None]).astype(BF16)
    sent = jnp.einsum(
        "sct,std->scd", place, rows.reshape(seq, tokens, width), preferred_element_type=F32
    ).astype(BF16).reshape(seq * cap, width)
    gate_part = jnp.dot(sent, w_gate[0], preferred_element_type=F32)
    up_part = jnp.dot(sent, w_up[0], preferred_element_type=F32)
    hidden = jax.nn.silu(gate_part) * up_part
    neuron_energy = unpruned(jnp.sum(hidden * hidden, axis=0))
    result = jnp.dot(hidden.astype(BF16), w_down[0], preferred_element_type=F32).astype(BF16)
    back = jnp.einsum(
        "sct,scd->std", place, result.reshape(seq, cap, width), preferred_element_type=F32
    )
    partial = (back * share[..., None]).astype(BF16).reshape(seq * tokens, width)
    moe = lax.psum_scatter(partial, "seq", scatter_dimension=0, tiled=True)
    mixed = residual_in.astype(F32) + moe.astype(F32)
    normed = (
        mixed * lax.rsqrt(jnp.mean(mixed * mixed, axis=-1, keepdims=True) + 1e-05) * norm_gain
    ).astype(BF16)
    query_width = QH * HD
    keys_vals = jnp.dot(normed, qkv_full[:, query_width:], preferred_element_type=F32).astype(BF16)
    kv = lax.all_gather(keys_vals, "seq", axis=0, tiled=True)
    queries = jnp.dot(normed, qkv_full[:, :query_width], preferred_element_type=F32).astype(BF16)
    attention = attention_call((queries * HD ** (-0.5)).T, kv)
    return (attention, neuron_energy)


def solution(mesh):
    return jax.shard_map(
        on_device,
        mesh=mesh,
        in_specs=(
            P(("groups", "seq"), None),
            P(("groups", "seq"), None),
            P(("groups", "seq"), None),
            P(("groups", "seq"), None),
            P("seq", None),
            P("seq", None, None),
            P("seq", None, None),
            P("seq", None, None),
            P(),
            P("seq", None),
        ),
        out_specs=(P(("groups", "seq"), None), P("seq", "groups")),
        check_vma=False,
    )
```

```python
import functools

import jax
import jax.numpy as jnp
from jax import lax
from jax.experimental import pallas as pl
from jax.experimental.pallas import tpu as pltpu
from jax.sharding import PartitionSpec as P

TOP = 4
BLOCK = 128
KB = 6
OB = 12
QH = 32
KVH = 4
HD = 64
BK = 256
QCHUNK = 512
F32 = jnp.float32
BF16 = jnp.bfloat16


def attention_kernel(qt_ref, kv_ref, out_ref, q_scr, m_scr, l_scr, acc_scr):
    me = lax.axis_index("seq")
    tokens = qt_ref.shape[1]
    heads = QCHUNK // tokens
    chunks = QH // heads
    for c in range(chunks):
        for h in range(heads):
            row = (c * heads + h) * HD
            q_scr[c, :, h * tokens : (h + 1) * tokens] = qt_ref[row : row + HD, :]
    m_scr[...] = jnp.full_like(m_scr, -1e30)
    l_scr[...] = jnp.zeros_like(l_scr)
    acc_scr[...] = jnp.zeros_like(acc_scr)

    def block(kb, masked):
        start = pl.multiple_of(kb * BK, BK)
        if masked:
            key_pos = start + lax.broadcasted_iota(jnp.int32, (BK, tokens), 0)
            query_pos = me * tokens + lax.broadcasted_iota(jnp.int32, (BK, tokens), 1)
            hide = jnp.where(key_pos <= query_pos, 0.0, -1e30)
            hide = jnp.concatenate([hide] * heads, axis=1)
        for c in range(chunks):
            g = c * heads // (QH // KVH)
            keys = kv_ref[pl.ds(start, BK), g * HD : (g + 1) * HD]
            vals = kv_ref[pl.ds(start, BK), (KVH + g) * HD : (KVH + g + 1) * HD]
            s = jnp.dot(keys, q_scr[c], preferred_element_type=F32)
            if masked:
                s = s + hide
            m_old = m_scr[c]
            m_new = jnp.maximum(m_old, jnp.max(s, axis=0, keepdims=True))
            p = jnp.exp(s - m_new)
            alpha = jnp.exp(m_old - m_new)
            m_scr[c] = m_new
            l_scr[c] = l_scr[c] * alpha + jnp.sum(p, axis=0, keepdims=True)
            pv = lax.dot_general(
                vals, p.astype(BF16), (((0,), (0,)), ((), ())), preferred_element_type=F32
            )
            acc_scr[c] = acc_scr[c] * alpha + pv

    full = me * tokens // BK

    @pl.loop(0, full)
    def _(kb):
        block(kb, False)

    block(full, True)
    for c in range(chunks):
        o = acc_scr[c] / l_scr[c]
        for h in range(0, heads, 2):
            pair = jnp.concatenate(
                [o[:, h * tokens : (h + 1) * tokens], o[:, (h + 1) * tokens : (h + 2) * tokens]], axis=0
            )
            col = (c * heads + h) * HD
            out_ref[:, col : col + 2 * HD] = pair.T.astype(BF16)


def attention_call(qt, kv):
    tokens = qt.shape[1]
    chunks = QH * tokens // QCHUNK
    return pl.pallas_call(
        attention_kernel,
        out_shape=jax.ShapeDtypeStruct((tokens, QH * HD), BF16),
        in_specs=[pl.BlockSpec(memory_space=pltpu.VMEM)] * 2,
        out_specs=pl.BlockSpec(memory_space=pltpu.VMEM),
        scratch_shapes=[
            pltpu.VMEM((chunks, HD, QCHUNK), BF16),
            pltpu.VMEM((chunks, 1, QCHUNK), F32),
            pltpu.VMEM((chunks, 1, QCHUNK), F32),
            pltpu.VMEM((chunks, HD, QCHUNK), F32),
        ],
        compiler_params=pltpu.CompilerParams(vmem_limit_bytes=40 * 1024 * 1024),
        name="attention",
    )(qt, kv)


MESH = pl.DeviceIdType.MESH


def position():
    me = lax.axis_index("seq")
    return me, me // 4, (me // 2) % 2, me % 2


def at(z, y, c):
    return (z * 2 + y) * 2 + c


def remote(src, dst, send_sem, recv_sem, target):
    return pltpu.make_async_remote_copy(
        src_ref=src,
        dst_ref=dst,
        send_sem=send_sem,
        recv_sem=recv_sem,
        device_id={"seq": target},
        device_id_type=MESH,
    )


def greet(rows):
    me, z, y, c = position()
    barrier = pltpu.get_barrier_semaphore()
    near = (
        at((z + 1) % rows, y, c),
        at((z + rows - 1) % rows, y, c),
        at(z, 1 - y, c),
        at(z, y, 1 - c),
    )
    for target in near:
        pl.semaphore_signal(barrier, inc=1, device_id={"seq": target}, device_id_type=MESH)
    pl.semaphore_wait(barrier, len(near))


def experts_kernel(
    rows, cap, x_ref, meta_ref, wq_ref, wg_ref, wu_ref, wd_ref,
    part_ref, energy_ref, wq_out, x_all, meta_all, sent, place_scr, local_sem, recv_sem, z_sem, y_sem, c_sem,
):
    me, z, y, c = position()
    last = rows - 1
    tokens, width = x_ref.shape
    half, whalf = width // 2, wq_ref.shape[1] // 2
    ins, outs = (x_ref, meta_ref, wq_ref), (x_all, meta_all, wq_out)
    parts = (
        (0, slice(0, half), True),
        (0, slice(half, width), False),
        (1, slice(0, tokens), True),
        (2, slice(0, whalf), True),
        (2, slice(whalf, 2 * whalf), False),
    )

    def own_copy(i):
        return pltpu.make_async_copy(ins[i], outs[i].at[me], local_sem.at[i])

    for i in range(3):
        own_copy(i).start()
    greet(rows)

    def copies(k, zz, yy, cc, own):
        i, cols, _ = parts[k]
        block = at(zz, yy, cc)
        src = ins[i].at[:, cols] if own else outs[i].at[block, :, cols]
        dst = outs[i].at[block, :, cols]
        got = recv_sem.at[k, block]
        line = zz * 2 + yy
        return {
            "up": lambda: remote(src, dst, z_sem.at[k, 0, line], got, at(lax.rem(z + 1, rows), y, c)),
            "down": lambda: remote(
                src, dst, z_sem.at[k, 1, line], got, at(lax.rem(z + last, rows), y, c)
            ),
            "y": lambda: remote(src, dst, y_sem.at[k, line], got, at(z, 1 - y, c)),
            "core": lambda: remote(src, dst, c_sem.at[k, line], got, at(z, y, 1 - c)),
        }

    def await_block(k, zz, yy, cc):
        copies(k, zz, yy, cc, False)["core"]().wait_recv()

    def act(verb, k, zz, yy, own, up, down, across):
        made = copies(k, zz, yy, c, own)
        if up:
            pl.when(z < last)(lambda: getattr(made["up"](), verb)())
        if down:
            pl.when(z > 0)(lambda: getattr(made["down"](), verb)())
        if across:
            getattr(made["y"](), verb)()
        getattr(made["core"](), verb)()

    def pass_on(*args):
        act("start", *args)

    def finish(*args):
        act("wait_send", *args)

    def walk_step(chosen, step, action, waiting):
        def reached(k, zz, yy, up, down, across):
            if waiting:
                await_block(k, zz, yy, c)
            action(k, zz, yy, False, up, down, across)

        if step == 0:
            for k in chosen:
                action(k, z, y, True, True, True, True)
            return
        if step == 1:
            for k in chosen:
                if not parts[k][2]:
                    reached(k, z, 1 - y, True, True, False)
        if step < rows:
            for k in chosen:
                z_first = parts[k][2]
                for yy in (y,) if z_first else (y, 1 - y):

                    @pl.when(z - step >= 0)
                    def _():
                        reached(k, z - step, yy, True, False, z_first)

                    @pl.when(z + step < rows)
                    def _():
                        reached(k, z + step, yy, False, True, z_first)

        for k in chosen:
            if parts[k][2]:
                if step == 1:
                    reached(k, z, 1 - y, False, False, False)
                else:

                    @pl.when(z - step + 1 >= 0)
                    def _():
                        reached(k, z - step + 1, 1 - y, False, False, False)

                    @pl.when(z + step - 1 < rows)
                    def _():
                        reached(k, z + step - 1, 1 - y, False, False, False)

    def from_core(chosen):
        for k in chosen:
            for zz in range(rows):
                for yy in range(2):
                    await_block(k, zz, yy, 1 - c)

    first, second = (2, 0, 1), (3, 4)
    for step in range(rows + 1):
        walk_step(first, step, pass_on, True)
        if step == 2:
            walk_step(second, 0, pass_on, True)
    from_core(first)
    walk_step(second, 1, pass_on, True)
    own_copy(0).wait()
    own_copy(1).wait()

    batch = 2 * 2
    earlier = (
        lax.broadcasted_iota(jnp.int32, (tokens, tokens), 0)
        < lax.broadcasted_iota(jnp.int32, (tokens, tokens), 1)
    ).astype(F32).astype(BF16)
    slots = lax.broadcasted_iota(jnp.int32, (cap, tokens), 0).astype(F32)
    mine = me.astype(F32)
    energy_ref[...] = jnp.zeros_like(energy_ref)
    for b in range(rows):
        shares = []
        for i in range(batch):
            block = b * batch + i
            meta = meta_all[block]
            hit = jnp.where(meta[:TOP] == mine, 1.0, 0.0)
            named = jnp.sum(hit, axis=0, keepdims=True)
            shares.append(jnp.sum(hit * meta[TOP:], axis=0, keepdims=True))
            slot = jnp.dot(
                jnp.broadcast_to(named, (16, tokens)).astype(BF16), earlier, preferred_element_type=F32
            )[:1]
            slot = jnp.where(named > 0.5, slot, -1.0)
            place = jnp.where(slots == slot, 1.0, 0.0).astype(BF16)
            place_scr[i] = place
            sent[i * cap : (i + 1) * cap, :] = jnp.dot(
                place, x_all[block], preferred_element_type=F32
            ).astype(BF16)
        gate_part = jnp.dot(sent[...], wg_ref[...], preferred_element_type=F32)
        up_part = jnp.dot(sent[...], wu_ref[...], preferred_element_type=F32)
        hidden = gate_part / (1.0 + jnp.exp(-gate_part)) * up_part
        energy_ref[...] += jnp.sum(hidden * hidden, axis=0, keepdims=True)
        result = jnp.dot(hidden.astype(BF16), wd_ref[...], preferred_element_type=F32).astype(BF16)
        for i in range(batch):
            back = lax.dot_general(
                place_scr[i],
                result[i * cap : (i + 1) * cap],
                (((0,), (0,)), ((), ())),
                preferred_element_type=F32,
            )
            share = jnp.broadcast_to(shares[i], (tokens, tokens)).T[:, :1]
            part_ref[b * batch + i] = (back * share).astype(BF16)
        if b + 2 <= rows:
            walk_step(second, b + 2, pass_on, True)
    from_core(second)
    for step in range(rows + 1):
        walk_step(first + second, step, finish, False)
    own_copy(2).wait()


def experts(x, meta, wq, wg, wu, wd, seq, cap):
    tokens, width = x.shape
    rows = seq // 4
    dma = pltpu.SemaphoreType.DMA
    return pl.pallas_call(
        functools.partial(experts_kernel, rows, cap),
        out_shape=[
            jax.ShapeDtypeStruct((seq, tokens, width), BF16),
            jax.ShapeDtypeStruct((1, wg.shape[1]), F32),
            jax.ShapeDtypeStruct((seq,) + wq.shape, BF16),
        ],
        in_specs=[pl.BlockSpec(memory_space=pltpu.VMEM)] * 6,
        out_specs=[pl.BlockSpec(memory_space=pltpu.VMEM)] * 3,
        scratch_shapes=[
            pltpu.VMEM((seq, tokens, width), BF16),
            pltpu.VMEM((seq, 2 * TOP, tokens), F32),
            pltpu.VMEM((4 * cap, width), BF16),
            pltpu.VMEM((4, cap, tokens), BF16),
            dma((3,)),
            dma((5, seq)),
            dma((5, 2, 2 * rows)),
            dma((5, 2 * rows)),
            dma((5, 2 * rows)),
        ],
        compiler_params=pltpu.CompilerParams(
            collective_id=0, has_side_effects=True, vmem_limit_bytes=56 * 1024 * 1024
        ),
        name="experts",
    )(x, meta, wq, wg, wu, wd)


def scatter_kernel(
    rows, part_ref, res_ref, gain_ref, out_ref, acc, c_buf, ya_buf, za_buf, zb_buf, yb_buf, mix,
    cs, cr, yas, yar, zas, zar, zbs, zbr, ybs, ybr,
):
    me, z, y, c = position()
    last = rows - 1
    half = part_ref.shape[2] // 2
    left, right = slice(0, half), slice(half, 2 * half)
    above, below = lax.rem(z + 1, rows), lax.rem(z + last, rows)
    other_y, other_c = at(z, 1 - y, c), at(z, y, 1 - c)
    greet(rows)
    order = []
    for i in range((rows + 1) // 2):
        order += [i] if i == last - i else [i, last - i]

    def core_copy(zz, yy):
        line = zz * 2 + yy
        return remote(part_ref.at[at(zz, yy, 1 - c)], c_buf.at[line], cs.at[line], cr.at[line], other_c)

    def ya_copy(zz):
        return remote(acc.at[zz * 2 + 1 - y, :, left], ya_buf.at[zz], yas.at[zz], yar.at[zz], other_y)

    def yb_copy():
        return remote(acc.at[z * 2 + 1 - y, :, right], yb_buf, ybs, ybr, other_y)

    def za_copy(zz, way):
        target = at(above if way == 0 else below, y, c)
        return remote(acc.at[zz * 2 + y, :, left], za_buf.at[way, zz], zas.at[zz], zar.at[way, zz], target)

    def zb_copy(zz, yy, way):
        target = at(above if way == 0 else below, y, c)
        line = zz * 2 + yy
        return remote(acc.at[line, :, right], zb_buf.at[way, line], zbs.at[line], zbr.at[way, line], target)

    def add(line, cols, value):
        acc[line, :, cols] = (acc[line, :, cols].astype(F32) + value.astype(F32)).astype(BF16)

    for zz in order:
        for yy in (1 - y, y):
            core_copy(zz, yy).start()
    for zz in order:
        for yy in (1 - y, y):
            line = zz * 2 + yy
            core_copy(zz, yy).wait_recv()
            acc[line] = (part_ref[at(zz, yy, c)].astype(F32) + c_buf[line].astype(F32)).astype(BF16)
            if zz < last:
                pl.when(z == last)(lambda: zb_copy(zz, yy, 1).start())
            if zz > 0:
                pl.when(z == 0)(lambda: zb_copy(zz, yy, 0).start())
        ya_copy(zz).start()
    for zz in order:

        def add_za(way):
            za_copy(zz, way).wait_recv()
            add(zz * 2 + y, left, za_buf[way, zz])

        def add_zb(yy, way):
            zb_copy(zz, yy, way).wait_recv()
            add(zz * 2 + yy, right, zb_buf[way, zz * 2 + yy])

        for yy in (1 - y, y):

            @pl.when((z > zz) & (z < last))
            def _():
                add_zb(yy, 1)
                zb_copy(zz, yy, 1).start()

            @pl.when((z < zz) & (z > 0))
            def _():
                add_zb(yy, 0)
                zb_copy(zz, yy, 0).start()

        ya_copy(zz).wait_recv()
        add(zz * 2 + y, left, ya_buf[zz])

        @pl.when(z > zz)
        def _():
            pl.when(z < last)(lambda: add_za(1))
            za_copy(zz, 1).start()

        @pl.when(z < zz)
        def _():
            pl.when(z > 0)(lambda: add_za(0))
            za_copy(zz, 0).start()

    for yy in (1 - y, y):
        line = z * 2 + yy

        @pl.when(z < last)
        def _():
            zb_copy(z, yy, 1).wait_recv()
            add(line, right, zb_buf[1, line])

        @pl.when(z > 0)
        def _():
            zb_copy(z, yy, 0).wait_recv()
            add(line, right, zb_buf[0, line])

    yb_copy().start()
    mine = z * 2 + y
    mix[:, left] = res_ref[:, left].astype(F32) + acc[mine, :, left].astype(F32)

    @pl.when(z < last)
    def _():
        za_copy(z, 1).wait_recv()
        mix[:, left] += za_buf[1, z].astype(F32)

    @pl.when(z > 0)
    def _():
        za_copy(z, 0).wait_recv()
        mix[:, left] += za_buf[0, z].astype(F32)

    yb_copy().wait_recv()
    mix[:, right] = res_ref[:, right].astype(F32) + (
        acc[mine, :, right].astype(F32) + yb_buf[...].astype(F32)
    )
    mixed = mix[...]
    scale = lax.rsqrt(jnp.mean(mixed * mixed, axis=-1, keepdims=True) + 1e-05)
    out_ref[...] = (mixed * scale * gain_ref[...]).astype(BF16)
    for zz in range(rows):
        for yy in range(2):
            core_copy(zz, yy).wait_send()
            pl.when(z > zz)(lambda: zb_copy(zz, yy, 1).wait_send())
            pl.when(z < zz)(lambda: zb_copy(zz, yy, 0).wait_send())
        ya_copy(zz).wait_send()
        pl.when(z > zz)(lambda: za_copy(zz, 1).wait_send())
        pl.when(z < zz)(lambda: za_copy(zz, 0).wait_send())
    yb_copy().wait_send()


def scatter_norm(partial, residual, gain, seq):
    _, tokens, width = partial.shape
    rows = seq // 4
    half = width // 2
    dma = pltpu.SemaphoreType.DMA
    return pl.pallas_call(
        functools.partial(scatter_kernel, rows),
        out_shape=jax.ShapeDtypeStruct((tokens, width), BF16),
        in_specs=[pl.BlockSpec(memory_space=pltpu.VMEM)] * 3,
        out_specs=pl.BlockSpec(memory_space=pltpu.VMEM),
        scratch_shapes=[
            pltpu.VMEM((2 * rows, tokens, width), BF16),
            pltpu.VMEM((2 * rows, tokens, width), BF16),
            pltpu.VMEM((rows, tokens, half), BF16),
            pltpu.VMEM((2, rows, tokens, half), BF16),
            pltpu.VMEM((2, 2 * rows, tokens, half), BF16),
            pltpu.VMEM((tokens, half), BF16),
            pltpu.VMEM((tokens, width), F32),
            dma((2 * rows,)),
            dma((2 * rows,)),
            dma((rows,)),
            dma((rows,)),
            dma((rows,)),
            dma((2, rows)),
            dma((2 * rows,)),
            dma((2, 2 * rows)),
            dma,
            dma,
        ],
        compiler_params=pltpu.CompilerParams(
            collective_id=2, has_side_effects=True, vmem_limit_bytes=48 * 1024 * 1024
        ),
        cost_estimate=pl.CostEstimate(flops=0, bytes_accessed=100_000_000, transcendentals=0),
        name="scatter_norm",
    )(partial, residual, gain.reshape(1, width))


def qkv_attention_kernel(
    rows, n_ref, w_ref, out_ref, kv_own, kv_all, q_scr, m_scr, l_scr, acc_scr, recv_sem, z_sem, y_sem, c_sem
):
    me, z, y, c = position()
    last = rows - 1
    tokens = n_ref.shape[0]
    query_width = QH * HD
    heads = QCHUNK // tokens
    chunks = QH // heads
    greet(rows)
    normed = n_ref[...]
    kv_own[...] = jnp.dot(normed, w_ref[:, query_width:], preferred_element_type=F32).astype(BF16)

    def place(zz, yy, cc):
        return kv_all.at[zz * 2 + yy, pl.ds(pl.multiple_of(cc * tokens, tokens), tokens), :]

    def copies(zz, yy, own):
        src = kv_own if own else place(zz, yy, c)
        dst = place(zz, yy, c)
        line = zz * 2 + yy
        got = recv_sem.at[at(zz, yy, c)]
        return {
            "up": lambda: remote(src, dst, z_sem.at[line], got, at(lax.rem(z + 1, rows), y, c)),
            "y": lambda: remote(src, dst, y_sem.at[line], got, at(z, 1 - y, c)),
            "core": lambda: remote(src, dst, c_sem.at[line], got, at(z, y, 1 - c)),
        }

    def await_block(zz, yy, cc):
        dst = place(zz, yy, cc)
        remote(dst, dst, c_sem.at[0], recv_sem.at[at(zz, yy, cc)], at(z, y, 1 - c)).wait_recv()

    def act(verb, zz, yy, own, along):
        made = copies(zz, yy, own)
        if along:
            pl.when(z < last)(lambda: getattr(made["up"](), verb)())
            getattr(made["y"](), verb)()
        getattr(made["core"](), verb)()

    act("start", z, y, True, True)
    kv_all[z * 2 + y, pl.ds(pl.multiple_of(c * tokens, tokens), tokens), :] = kv_own[...]
    m_scr[...] = jnp.full_like(m_scr, -1e30)
    l_scr[...] = jnp.zeros_like(l_scr)
    acc_scr[...] = jnp.zeros_like(acc_scr)
    step_cols = QCHUNK // tokens * HD
    for ch in range(chunks):
        q = jnp.dot(
            normed, w_ref[:, ch * step_cols : (ch + 1) * step_cols], preferred_element_type=F32
        )
        q = q.astype(BF16).astype(F32) * HD ** (-0.5)
        for h in range(0, heads, 2):
            pair = q[:, h * HD : (h + 2) * HD].T.astype(BF16)
            q_scr[ch, :, h * tokens : (h + 1) * tokens] = pair[:HD]
            q_scr[ch, :, (h + 1) * tokens : (h + 2) * tokens] = pair[HD:]

    def block(line, masked):
        if masked:
            key_pos = lax.broadcasted_iota(jnp.int32, (BK, tokens), 0)
            query_pos = c * tokens + lax.broadcasted_iota(jnp.int32, (BK, tokens), 1)
            hide = jnp.where(key_pos <= query_pos, 0.0, -1e30)
            hide = jnp.concatenate([hide] * heads, axis=1)
        for ch in range(chunks):
            g = ch * heads // (QH // KVH)
            keys = kv_all[line, :, g * HD : (g + 1) * HD]
            vals = kv_all[line, :, (KVH + g) * HD : (KVH + g + 1) * HD]
            s = jnp.dot(keys, q_scr[ch], preferred_element_type=F32)
            if masked:
                s = s + hide
            m_old = m_scr[ch]
            m_new = jnp.maximum(m_old, jnp.max(s, axis=0, keepdims=True))
            p = jnp.exp(s - m_new)
            alpha = jnp.exp(m_old - m_new)
            m_scr[ch] = m_new
            l_scr[ch] = l_scr[ch] * alpha + jnp.sum(p, axis=0, keepdims=True)
            pv = lax.dot_general(
                vals, p.astype(BF16), (((0,), (0,)), ((), ())), preferred_element_type=F32
            )
            acc_scr[ch] = acc_scr[ch] * alpha + pv

    def relay(zz, yy, along):
        await_block(zz, yy, c)
        act("start", zz, yy, False, along)

    relay(z, 1 - y, False)
    pl.when(z >= 1)(lambda: relay(z - 1, y, True))
    await_block(z, y, 1 - c)
    block(z * 2 + y, True)
    for step in range(1, rows + 1):
        if step < last:
            pl.when(z >= step + 1)(lambda: relay(z - step - 1, y, True))
        if step <= last:
            pl.when(z >= step)(lambda: relay(z - step, 1 - y, False))
        back = step - 1

        @pl.when(z >= back)
        def _():
            await_block(z - back, 1 - y, 1 - c)
            if back > 0:
                await_block(z - back, y, 1 - c)

        if back == 0:
            pl.when(y == 1)(lambda: block(z * 2, False))
        else:

            @pl.when(z >= back)
            def _():
                @pl.loop(0, 2)
                def _(yy):
                    block((z - back) * 2 + yy, False)

    for ch in range(chunks):
        o = acc_scr[ch] / l_scr[ch]
        for h in range(0, heads, 2):
            pair = jnp.concatenate(
                [o[:, h * tokens : (h + 1) * tokens], o[:, (h + 1) * tokens : (h + 2) * tokens]], axis=0
            )
            col = (ch * heads + h) * HD
            out_ref[:, col : col + 2 * HD] = pair.T.astype(BF16)
    act("wait_send", z, y, True, True)
    act("wait_send", z, 1 - y, False, False)
    for back in range(1, rows):
        pl.when(z >= back)(lambda: act("wait_send", z - back, y, False, True))
        pl.when(z >= back)(lambda: act("wait_send", z - back, 1 - y, False, False))


def qkv_attention(normed, weight, seq):
    tokens = normed.shape[0]
    chunks = QH * tokens // QCHUNK
    rows = seq // 4
    dma = pltpu.SemaphoreType.DMA
    return pl.pallas_call(
        functools.partial(qkv_attention_kernel, rows),
        out_shape=jax.ShapeDtypeStruct((tokens, QH * HD), BF16),
        in_specs=[pl.BlockSpec(memory_space=pltpu.VMEM)] * 2,
        out_specs=pl.BlockSpec(memory_space=pltpu.VMEM),
        scratch_shapes=[
            pltpu.VMEM((tokens, 2 * KVH * HD), BF16),
            pltpu.VMEM((2 * rows, 2 * tokens, 2 * KVH * HD), BF16),
            pltpu.VMEM((chunks, HD, QCHUNK), BF16),
            pltpu.VMEM((chunks, 1, QCHUNK), F32),
            pltpu.VMEM((chunks, 1, QCHUNK), F32),
            pltpu.VMEM((chunks, HD, QCHUNK), F32),
            dma((seq,)),
            dma((2 * rows,)),
            dma((2 * rows,)),
            dma((2 * rows,)),
        ],
        compiler_params=pltpu.CompilerParams(
            collective_id=1, has_side_effects=True, vmem_limit_bytes=48 * 1024 * 1024
        ),
        name="qkv_attention",
    )(normed, weight)


def on_device(
    moe_input,
    residual_in,
    expert_ids,
    route_logits,
    kept_blocks,
    w_gate,
    w_up,
    w_down,
    norm_gain,
    qkv_weight,
):
    tokens, width = moe_input.shape
    seq = lax.axis_size("seq")
    me = lax.axis_index("seq")
    cap = min(tokens, max(2, tokens * TOP * 2 // seq))
    raised = jnp.exp(route_logits)
    weights = raised / jnp.sum(raised, axis=-1, keepdims=True)
    chosen = (kept_blocks[0][:, None] == jnp.arange(OB, dtype=jnp.int32)[None, :]).astype(F32)

    def unpruned(squares):
        energy = jnp.sqrt(squares / (seq * cap) + 1e-06)
        placed = jnp.einsum(
            "bo,bc->oc", chosen, energy.reshape(KB, BLOCK), precision=lax.Precision.HIGHEST
        )
        return placed.reshape(1, OB * BLOCK)

    meta = jnp.concatenate([expert_ids.astype(F32), weights], axis=1)
    if seq == 16 and tokens == 128:
        partial, squares, qkv_full = experts(
            moe_input, meta.T, qkv_weight, w_gate[0], w_up[0], w_down[0], seq, cap
        )
        normed = scatter_norm(partial, residual_in, norm_gain, seq)
        attention = qkv_attention(normed, qkv_full.reshape(width, -1), seq)
        return (attention, unpruned(squares))
    meta = lax.all_gather(meta, "seq", axis=0, tiled=True)
    rows = lax.all_gather(moe_input, "seq", axis=0, tiled=True)
    qkv_full = lax.all_gather(qkv_weight, "seq", axis=0, tiled=True)

    hit = (meta[:, :TOP] == me.astype(F32)).astype(F32)
    share = jnp.sum(hit * meta[:, TOP:], axis=1).reshape(seq, tokens)
    named = jnp.sum(hit, axis=1).reshape(seq, tokens)
    earlier = (jnp.arange(tokens)[:, None] < jnp.arange(tokens)[None, :]).astype(F32)
    slot = jnp.dot(named, earlier)
    slot = jnp.where(named > 0.5, slot, -1.0)
    place = (slot[:, None, :] == jnp.arange(cap, dtype=F32)[None, :, None]).astype(BF16)
    sent = jnp.einsum(
        "sct,std->scd", place, rows.reshape(seq, tokens, width), preferred_element_type=F32
    ).astype(BF16).reshape(seq * cap, width)
    gate_part = jnp.dot(sent, w_gate[0], preferred_element_type=F32)
    up_part = jnp.dot(sent, w_up[0], preferred_element_type=F32)
    hidden = jax.nn.silu(gate_part) * up_part
    neuron_energy = unpruned(jnp.sum(hidden * hidden, axis=0))
    result = jnp.dot(hidden.astype(BF16), w_down[0], preferred_element_type=F32).astype(BF16)
    back = jnp.einsum(
        "sct,scd->std", place, result.reshape(seq, cap, width), preferred_element_type=F32
    )
    partial = (back * share[..., None]).astype(BF16).reshape(seq * tokens, width)
    moe = lax.psum_scatter(partial, "seq", scatter_dimension=0, tiled=True)
    mixed = residual_in.astype(F32) + moe.astype(F32)
    normed = (
        mixed * lax.rsqrt(jnp.mean(mixed * mixed, axis=-1, keepdims=True) + 1e-05) * norm_gain
    ).astype(BF16)
    query_width = QH * HD
    keys_vals = jnp.dot(normed, qkv_full[:, query_width:], preferred_element_type=F32).astype(BF16)
    kv = lax.all_gather(keys_vals, "seq", axis=0, tiled=True)
    queries = jnp.dot(normed, qkv_full[:, :query_width], preferred_element_type=F32).astype(BF16)
    attention = attention_call((queries * HD ** (-0.5)).T, kv)
    return (attention, neuron_energy)


def solution(mesh):
    return jax.shard_map(
        on_device,
        mesh=mesh,
        in_specs=(
            P(("groups", "seq"), None),
            P(("groups", "seq"), None),
            P(("groups", "seq"), None),
            P(("groups", "seq"), None),
            P("seq", None),
            P("seq", None, None),
            P("seq", None, None),
            P("seq", None, None),
            P(),
            P("seq", None),
        ),
        out_specs=(P(("groups", "seq"), None), P("seq", "groups")),
        check_vma=False,
    )
```
